256 devices in a mesh: depth: 4 (over x), tile: 64 (over z, y, core).
Axes of the slice: x: 4, y: 4, z: 8, core: 2. Of those that a mesh axis runs over, the one named last changes fastest.
Arguments:
- density: bfloat16 [128, 4096, 2048], P('depth', 'tile'), may hold values from 0 to 2
- depth_rank: int32 [4], replicated, may hold values from 0 to 3, as said below
- piece_home: int32 [4096], P('tile'), may hold values from 0 to 4095, as said below
Outputs:
- display: float32 [3, 4, 4096, 512], P(None, 'depth', 'tile')
The draws below stay inside these ranges and needn't reach their ends.
Inputs may be any that keep to these rules, and one draw needn't show every extreme that they name: Either depth_rank[i] = i for every i, or depth_rank[i] = 3 - i for every i. `piece_home`: every value appears exactly once. A value h names slot h % 64 of the device h // 64 along tile. The number of the 64 entries of tile device s that name device o depends only on (o - s) mod 64, is at most 2, and equals 2 for some pair.
All inputs are finite; a program needn't handle non-finite values.
Results may differ from the reference program's by a relative error of at most 0.0003.
Values may be sent and summed in bfloat16 or wider, within the bound.
No kernel may reach another device: no remote copies, remote signals or barrier semaphores. Data moves between devices by JAX's collectives and lax.ppermute only.
A program may use at most 128 MiB of HBM per device.

```python
import math
from functools import partial
import jax
import jax.numpy as jnp
from jax import lax

CZ = 32
BY = 64
IMAGE_COLUMNS = 2048
VIEW_CELLS = 128
IMAGE_ROWS = 4096
PPD = 64
PR = 512
PIECES = 4096
N_DEPTH = 4
N_TILE = 64


def draw_density(key, part):
    random_keys = jax.random.split(key, 4)
    low_end, high_end = (0.003, 0.25)
    logs = jax.random.uniform(random_keys[0], (1, IMAGE_ROWS, IMAGE_COLUMNS), jnp.float32, math.log(low_end), math.log(high_end))
    column_weighting = jnp.exp(logs)
    surface_bumpiness = jax.random.uniform(random_keys[1], (VIEW_CELLS, IMAGE_ROWS, IMAGE_COLUMNS), jnp.float32, 0.5, 1.5)
    spike_row_indices = jax.random.randint(random_keys[2], (3,), 0, VIEW_CELLS)
    slice_depth_index = jnp.arange(VIEW_CELLS)
    spike_active = jnp.any(slice_depth_index[:, None] == spike_row_indices[None, :], axis=1).astype(jnp.float32)
    spike_multiplier = jax.random.uniform(random_keys[3], (1, IMAGE_ROWS, IMAGE_COLUMNS), jnp.float32, 0.5, 1.5)
    solute_field_value = column_weighting * surface_bumpiness + 0.7 * spike_active[:, None, None] * spike_multiplier
    return solute_field_value.astype(jnp.bfloat16)


def draw_depth_rank(key, part):
    brick_count = VIEW_CELLS // CZ
    flipped = jax.random.randint(key, (), 0, 2)
    positions = jnp.arange(brick_count)
    return jnp.where(flipped == 1, brick_count - 1 - positions, positions).astype(jnp.int32)


def draw_piece_home(key, part):
    tile_count = IMAGE_ROWS // BY
    random_keys = jax.random.split(key, 4)
    doubles = jax.random.randint(random_keys[0], (), 1, tile_count // 2 + 1)
    shuffle = jax.random.permutation(random_keys[1], tile_count)
    counts = jnp.where(shuffle < doubles, 2, jnp.where(shuffle < 2 * doubles, 0, 1)).astype(jnp.int32)
    bounds = jnp.cumsum(counts)
    permuter = jax.vmap(partial(jax.random.permutation, x=PPD))
    ranks = permuter(jax.random.split(random_keys[2], tile_count)).astype(jnp.int32)
    offsets = jnp.sum((bounds[None, None, :] <= ranks[:, :, None]).astype(jnp.int32), axis=2)
    owners = (jnp.arange(tile_count, dtype=jnp.int32)[:, None] + offsets) % tile_count
    slots = permuter(jax.random.split(random_keys[3], tile_count)).astype(jnp.int32)
    homes = owners * PPD + slots[owners, ranks]
    return homes.reshape(-1).astype(jnp.int32)


def setup_inputs(seed: int = 0) -> dict:
    arg_keys = jax.random.split(jax.random.key(seed), 4)
    density = draw_density(jax.random.fold_in(arg_keys[3], 71), 0)
    depth_rank = draw_depth_rank(jax.random.fold_in(arg_keys[3], 71), 0)
    piece_home = draw_piece_home(jax.random.fold_in(arg_keys[3], 71), 0)
    return {"density": density, "depth_rank": depth_rank, "piece_home": piece_home}


EXTINCT = 0.5
LIGHT_Z = 0.6
LIGHT_Y = 0.48
LIGHT_X = 0.64
SHARPNESS = 6.0
BACKDROP = (0.08, 0.1, 0.14)


def lighting(padded):
    center = padded[1:-1, 1:-1, :]
    grad_z = 0.5 * (padded[2:, 1:-1, :] - padded[:-2, 1:-1, :])
    grad_y = 0.5 * (padded[1:-1, 2:, :] - padded[1:-1, :-2, :])
    padded_x = jnp.pad(center, ((0, 0), (0, 0), (1, 1)))
    grad_x = 0.5 * (padded_x[:, :, 2:] - padded_x[:, :, :-2])
    facing = LIGHT_Z * grad_z + LIGHT_Y * grad_y + LIGHT_X * grad_x
    shading = 0.35 + 0.65 * (0.5 + 0.5 * jnp.tanh(SHARPNESS * facing))
    return center, shading


def emission(center):
    logged = jnp.log(center + 0.01)
    return (jax.nn.sigmoid(logged + 3.0), 0.5 + 0.5 * jnp.cos(1.7 * logged), jax.nn.sigmoid(-(logged + 2.5)))


def reference(density, depth_rank, piece_home):
    ascend = depth_rank[0] == 0
    padded = jnp.pad(density, ((1, 1), (1, 1), (0, 0)))
    backdrop = jnp.array(BACKDROP, jnp.float32)[:, None, None]

    def one_block(block_index):
        first_row = (block_index * BY).astype(jnp.int32)
        window = lax.dynamic_slice_in_dim(padded, first_row, BY + 2, 1).astype(jnp.float32)
        center, shading = lighting(window)
        optical = EXTINCT * center
        forward = lax.cumsum(optical, 0) - optical
        backward = lax.cumsum(optical, 0, reverse=True) - optical
        before = jnp.where(ascend, forward, backward)
        weight = jnp.exp(-before) * (-jnp.expm1(-optical)) * shading
        colors = emission(center)
        radiance = jnp.stack([jnp.sum(weight * channel, axis=0) for channel in colors])
        through = jnp.exp(-jnp.sum(optical, axis=0))
        return radiance + through[None] * backdrop

    finals = lax.map(one_block, jnp.arange(N_TILE, dtype=jnp.int32))
    pieces = finals.reshape(N_TILE, 3, N_DEPTH, PPD, PR)
    pieces = pieces.transpose(1, 2, 0, 3, 4).reshape(3, N_DEPTH, PIECES, PR)
    display = jnp.zeros_like(pieces).at[:, :, piece_home, :].set(pieces)
    return display
```

```python
import functools
import math

import jax
import jax.numpy as jnp
import numpy as np
from jax import lax
from jax.experimental import pallas as pl
from jax.experimental.pallas import tpu as pltpu
from jax.sharding import PartitionSpec as P

EXTINCT = 0.5
BACKDROP = (0.08, 0.1, 0.14)
CODE = 65535.0

XB = 256
PIECE = 512
HALF = PIECE // 2
PAYLOAD = 3 * HALF
ROW_WORDS = 2 * PAYLOAD + 128


def cosine_polynomial(degree):
    limit = (0.85 * math.log(0.01) + math.pi / 2) ** 2 * 1.0005
    nodes = np.cos(np.pi * (np.arange(4000) + 0.5) / 4000)
    points = (nodes + 1) * limit / 2
    fit = np.polynomial.chebyshev.Chebyshev.fit(
        points, np.cos(np.sqrt(points)), degree, domain=[0, limit]
    )
    return [float(c) for c in fit.convert(kind=np.polynomial.Polynomial).coef]


COS = cosine_polynomial(4)


def difference_matrices(rows):
    along_x = np.zeros((XB, XB))
    j = np.arange(XB - 1)
    along_x[j + 1, j] = 16
    along_x[j, j + 1] = -16
    beside = np.zeros((3, XB, XB))
    beside[1:, 127, 0] = -16
    beside[:2, 128, XB - 1] = 16
    along_zy = np.zeros((2 * rows, 4 * rows))
    y = np.arange(rows)
    for b in range(2):
        out, center = b * rows, (b + 1) * rows
        along_zy[out + y, center + rows + y] += 15
        along_zy[out + y, center - rows + y] -= 15
        along_zy[out + y[:-1], center + y[1:]] += 12
        along_zy[out + y[1:], center + y[:-1]] -= 12
    return [jnp.asarray(v, jnp.bfloat16) for v in (along_zy, along_x, beside)]


def dot(a, b):
    return jnp.dot(a, b, preferred_element_type=jnp.float32)


def encode(value):
    return (value * CODE + 0.5).astype(jnp.int32)


def march_kernel(
    rank, cells, left, right, below, above, front, back, along_zy, along_x, beside, *rest
):
    outs, slope = rest[:-1], rest[-1]
    depth, rows, _ = cells.shape
    quarters = len(outs)
    band = rows // quarters
    chunk = 8
    for first in range(0, depth, chunk):
        part = slice(first, first + chunk)
        sides = jnp.concatenate(
            [left[part].reshape(chunk * rows, 128), right[part].reshape(chunk * rows, 128)], 1
        )
        inner = cells[part].reshape(chunk * rows, XB)
        slope[part] = (dot(inner, along_x[...]) + dot(sides, beside[0])).reshape(chunk, rows, XB)
    for first in range(0, depth, 2):
        low = below[...] if first == 0 else cells[first - 1 : first]
        high = above[...] if first + 2 == depth else cells[first + 2 : first + 3]
        stack = jnp.concatenate([low, cells[first : first + 2], high], 0)
        part = dot(along_zy[...], stack.reshape(4 * rows, XB))
        slope[first : first + 2] += part.reshape(2, rows, XB)
    slope[:, :1, :] -= 12.0 * front[...].astype(jnp.float32)
    slope[:, rows - 1 :, :] += 12.0 * back[...].astype(jnp.float32)

    ascend = rank[0] == 0
    me = lax.axis_index("depth")
    lead = COS[4]
    c3, c2, c1, c0 = [COS[i] / lead for i in (3, 2, 1, 0)]
    for k in range(quarters):
        row = pl.multiple_of(lax.rem(me + k, quarters) * band, band)
        zero = jnp.zeros((band, XB), jnp.float32)

        def step(i, carry):
            total, clear, plain, sum0, sum1, sum2 = carry
            z = jnp.where(ascend, i, depth - 1 - i)
            density = cells[z, pl.ds(row, band), :].astype(jnp.float32)
            facing = jnp.tanh(0.12 * slope[z, pl.ds(row, band), :])
            total = total + density
            after = jnp.exp(-EXTINCT * total)
            weight = (clear - after) * (facing + 0.675 / 0.325)
            logged = jnp.log(density + 0.01)
            psi = 0.85 * logged + math.pi / 2
            half = 0.5 * logged + 1.5
            square = psi * psi
            cosine = (((square + c3) * square + c2) * square + c1) * square + c0
            return (
                total,
                after,
                plain + weight,
                sum0 + weight * jnp.tanh(half),
                sum1 + weight * (cosine * cosine),
                sum2 + weight * jnp.tanh(half - 0.25),
            )

        _, through, plain, sum0, sum1, sum2 = lax.fori_loop(
            0, depth, step, (zero, zero + 1.0, zero, zero, zero, zero), unroll=8
        )
        plain = 0.325 * plain
        color0 = 0.5 * plain + 0.1625 * sum0
        color1 = plain - (0.325 * lead * lead) * sum1
        color2 = 0.5 * plain - 0.1625 * sum2
        outs[k][0] = encode(color0) + (encode(color1) << 16)
        outs[k][1] = encode(color2) + (encode(through) << 16)


def march(depth_rank, density, below, above, front, back, quarters):
    depth, rows, columns = density.shape
    blocks = columns // XB
    constants = difference_matrices(rows)
    in_specs = [
        pl.BlockSpec(memory_space=pltpu.SMEM),
        pl.BlockSpec((depth, rows, XB), lambda i: (0, 0, i)),
        pl.BlockSpec((depth, rows, 128), lambda i: (0, 0, jnp.maximum(2 * i - 1, 0))),
        pl.BlockSpec((depth, rows, 128), lambda i: (0, 0, jnp.minimum(2 * i + 2, 2 * blocks - 1))),
        pl.BlockSpec((1, rows, XB), lambda i: (0, 0, i)),
        pl.BlockSpec((1, rows, XB), lambda i: (0, 0, i)),
        pl.BlockSpec((depth, 1, XB), lambda i: (0, 0, i)),
        pl.BlockSpec((depth, 1, XB), lambda i: (0, 0, i)),
        pl.BlockSpec((2 * rows, 4 * rows), lambda i: (0, 0)),
        pl.BlockSpec((XB, XB), lambda i: (0, 0)),
        pl.BlockSpec(
            (1, XB, XB),
            lambda i: (jnp.where(i == 0, 0, jnp.where(i == blocks - 1, 2, 1)), 0, 0),
        ),
    ]
    return pl.pallas_call(
        march_kernel,
        grid=(blocks,),
        in_specs=in_specs,
        out_specs=[pl.BlockSpec((2, rows // quarters, XB), lambda i: (0, 0, i))] * quarters,
        out_shape=[jax.ShapeDtypeStruct((2, rows // quarters, columns), jnp.int32)] * quarters,
        scratch_shapes=[pltpu.VMEM((depth, rows, XB), jnp.float32)],
        compiler_params=pltpu.CompilerParams(vmem_limit_bytes=40 * 2**20),
        name="march",
    )(depth_rank, density, density, density, below, above, front, back, *constants)


def decode(words):
    low = (words & 65535).astype(jnp.float32) * (1.0 / CODE)
    high = ((words >> 16) & 65535).astype(jnp.float32) * (1.0 / CODE)
    return low, high


def tile_bytes(value):
    code = jnp.floor(value * CODE + 0.5)
    high = jnp.floor(code * (1.0 / 256.0))
    return high.astype(jnp.bfloat16), (code - 256.0 * high).astype(jnp.bfloat16)


def gather_kernel(rank, home, *refs):
    bricks, out = refs[:-1], refs[-1]
    members = len(bricks)
    _, band, columns = bricks[0].shape
    across = columns // PIECE
    count = band * across
    ascend = rank[0] == 0
    me = lax.axis_index("depth")
    places = []
    for k in range(members):
        index = lax.rem(me - k + members, members)
        places.append(jnp.where(ascend, index, members - 1 - index))

    piece = lax.broadcasted_iota(jnp.int32, (count, count), 0)
    column = lax.broadcasted_iota(jnp.int32, (count, count), 1)
    homes = home[...]
    regroup = (piece == lax.rem(column, band) * across + column // band).astype(jnp.bfloat16)
    named = (piece == (homes // count)).astype(jnp.bfloat16)
    earlier = dot(named, (piece < column).astype(jnp.bfloat16))
    slots = (homes % count + 1).astype(jnp.float32)
    label = jnp.zeros((count, 128), jnp.int32)
    lane = lax.broadcasted_iota(jnp.int32, (count, 128), 1)
    routes = []
    for e in range(2):
        chosen = named.astype(jnp.float32) * (earlier == float(e)).astype(jnp.float32)
        here = jnp.sum(chosen * slots, axis=1, keepdims=True).astype(jnp.int32)
        label = label + jnp.where(lane == e, here, 0)
        routes.append(dot(chosen.astype(jnp.bfloat16), regroup).astype(jnp.bfloat16))
    out[:, 2 * PAYLOAD :] = label

    planes = [[], [], []]
    for c in range(across):
        part = slice(c * PIECE, (c + 1) * PIECE)
        colors, clears = [], []
        for brick in bricks:
            first, second = decode(brick[0, :, part])
            third, clear = decode(brick[1, :, part])
            colors.append((first, second, third))
            clears.append(clear)
        total = clears[0]
        for clear in clears[1:]:
            total = total * clear
        done = [total * b for b in BACKDROP]
        for k in range(members):
            ahead = None
            for other in range(members):
                if other != k:
                    factor = jnp.where(places[other] < places[k], clears[other], 1.0)
                    ahead = factor if ahead is None else ahead * factor
            done = [d + ahead * color for d, color in zip(done, colors[k])]
        for channel in range(3):
            planes[channel].append(tile_bytes(done[channel]))
    for channel in range(3):
        high = jnp.concatenate([p[0] for p in planes[channel]], 0)
        low = jnp.concatenate([p[1] for p in planes[channel]], 0)
        for e in range(2):
            code = (256.0 * dot(routes[e], high) + dot(routes[e], low)).astype(jnp.int32)
            words = code[:, :HALF] + (code[:, HALF:] << 16)
            at = e * PAYLOAD + channel * HALF
            out[:, at : at + HALF] = words


def gather(depth_rank, piece_home, bricks):
    _, band, columns = bricks[0].shape
    count = piece_home.shape[0]
    vmem = pl.BlockSpec(memory_space=pltpu.VMEM)
    return pl.pallas_call(
        gather_kernel,
        in_specs=[pl.BlockSpec(memory_space=pltpu.SMEM)] + [vmem] * (1 + len(bricks)),
        out_specs=vmem,
        out_shape=jax.ShapeDtypeStruct((count, ROW_WORDS), jnp.int32),
        compiler_params=pltpu.CompilerParams(vmem_limit_bytes=24 * 2**20),
        name="gather",
    )(depth_rank, piece_home.reshape(1, count), *bricks)


def place_kernel(arrived, out):
    count = arrived.shape[0]
    slot = lax.broadcasted_iota(jnp.int32, (count, count), 1)
    choices = [
        (arrived[:, 2 * PAYLOAD + e : 2 * PAYLOAD + e + 1] == slot + 1).astype(jnp.bfloat16)
        for e in range(2)
    ]
    choice = jnp.concatenate(choices, 0)

    def plane(words, shift):
        return ((words >> shift) & 255).astype(jnp.float32).astype(jnp.bfloat16)

    def put(planes):
        return lax.dot_general(
            choice, planes, (((0,), (0,)), ((), ())), preferred_element_type=jnp.float32
        )

    for channel in range(3):
        at = channel * HALF
        words = jnp.concatenate(
            [arrived[:, e * PAYLOAD + at : e * PAYLOAD + at + HALF] for e in range(2)], 0
        )
        for half in range(2):
            code = 256.0 * put(plane(words, 16 * half + 8)) + put(plane(words, 16 * half))
            out[channel, 0, :, half * HALF : (half + 1) * HALF] = code * (1.0 / CODE)


def place(arrived):
    count = arrived.shape[0]
    vmem = pl.BlockSpec(memory_space=pltpu.VMEM)
    return pl.pallas_call(
        place_kernel,
        in_specs=[vmem],
        out_specs=vmem,
        out_shape=jax.ShapeDtypeStruct((3, 1, count, PIECE), jnp.float32),
        compiler_params=pltpu.CompilerParams(vmem_limit_bytes=24 * 2**20),
        name="place",
    )(arrived)


def neighbors(shard, axis, dim):
    peers, length = lax.axis_size(axis), shard.shape[dim]
    up = [(i, i + 1) for i in range(peers - 1)]
    last = lax.slice_in_dim(shard, length - 1, length, axis=dim)
    first = lax.slice_in_dim(shard, 0, 1, axis=dim)
    return lax.ppermute(last, axis, up), lax.ppermute(first, axis, [(b, a) for a, b in up])


def on_device(density, depth_rank, piece_home):
    members = lax.axis_size("depth")
    below, above = neighbors(density, "depth", 0)
    front, back = neighbors(density, "tile", 1)
    parts = march(depth_rank, density, below, above, front, back, members)
    bricks = [parts[0]]
    for k in range(1, members):
        ring = [(i, (i + k) % members) for i in range(members)]
        bricks.append(lax.ppermute(parts[k], "depth", ring))
    outbox = gather(depth_rank, piece_home, bricks)
    arrived = lax.all_to_all(outbox, "tile", split_axis=0, concat_axis=0, tiled=True)
    return place(arrived)


def solution(mesh):
    in_specs = (P("depth", "tile", None), P(), P("tile"))
    out_specs = P(None, "depth", "tile", None)
    return jax.shard_map(
        on_device, mesh=mesh, in_specs=in_specs, out_specs=out_specs, check_vma=False
    )
```

```python
import functools
import math

import jax
import jax.numpy as jnp
import numpy as np
from jax import lax
from jax.experimental import pallas as pl
from jax.experimental.pallas import tpu as pltpu
from jax.sharding import PartitionSpec as P

EXTINCT = 0.5
BACKDROP = (0.08, 0.1, 0.14)
CODE = 65535.0

XB = 256
PIECE = 512
HALF = PIECE // 2
PAYLOAD = 3 * HALF
ROW_WORDS = 2 * PAYLOAD + 128


def cosine_polynomial(degree):
    limit = (0.85 * math.log(0.01) + math.pi / 2) ** 2 * 1.0005
    nodes = np.cos(np.pi * (np.arange(4000) + 0.5) / 4000)
    points = (nodes + 1) * limit / 2
    fit = np.polynomial.chebyshev.Chebyshev.fit(
        points, np.cos(np.sqrt(points)), degree, domain=[0, limit]
    )
    return [float(c) for c in fit.convert(kind=np.polynomial.Polynomial).coef]


COS = cosine_polynomial(4)
SHIFT = math.exp(math.pi / 1.7)
OFFSET = 0.01 * SHIFT
EXTINCT2 = -0.5 * math.log2(math.e) / SHIFT
NEAR = SHIFT * math.exp(-3.0)
FAR = SHIFT * math.exp(-2.5)
MONIC = [COS[i] / COS[4] / 0.85 ** (8 - 2 * i) for i in range(4)]
COSINE_SCALE = (COS[4] * 0.85**8) ** 2


def difference_matrices(rows):
    along_x = np.zeros((XB, XB))
    j = np.arange(XB - 1)
    along_x[j + 1, j] = 16
    along_x[j, j + 1] = -16
    beside = np.zeros((3, XB, XB))
    beside[1:, 127, 0] = -16
    beside[:2, 128, XB - 1] = 16
    along_zy = np.zeros((2 * rows, 4 * rows))
    y = np.arange(rows)
    for b in range(2):
        out, center = b * rows, (b + 1) * rows
        along_zy[out + y, center + rows + y] += 15
        along_zy[out + y, center - rows + y] -= 15
        along_zy[out + y[:-1], center + y[1:]] += 12
        along_zy[out + y[1:], center + y[:-1]] -= 12
    return [jnp.asarray(v, jnp.bfloat16) for v in (along_zy, along_x, beside)]


def dot(a, b):
    return jnp.dot(a, b, preferred_element_type=jnp.float32)


def encode(value):
    return (value * CODE + 0.5).astype(jnp.int32)


def shade(facing_sum, density, weight):
    weight = weight * (jnp.tanh(0.12 * facing_sum) + 0.675 / 0.325)
    logged = jnp.log(density + OFFSET)
    square = logged * logged
    c0, c1, c2, c3 = MONIC
    cosine = (((square + c3) * square + c2) * square + c1) * square + c0
    near = pltpu.reciprocal(density + (OFFSET + NEAR))
    far = pltpu.reciprocal(density + (OFFSET + FAR))
    return weight, weight * near, weight * (cosine * cosine), weight * far


def colors_of(plain, sum0, sum1, sum2):
    plain = 0.325 * plain
    return plain - (0.325 * NEAR) * sum0, plain - (0.325 * COSINE_SCALE) * sum1, (0.325 * FAR) * sum2


def scaled(cells):
    return SHIFT * cells.astype(jnp.float32)


def march(cell, slope, ascend, first, last, start, unroll):
    def step(i, carry):
        total, clear, *sums = carry
        z = jnp.where(ascend, first + i, last - i)
        density = cell(z)
        total = total + density
        after = jnp.exp2(EXTINCT2 * total)
        terms = shade(slope(z), density, clear - after)
        return (total, after, *(s + t for s, t in zip(sums, terms)))

    zero = jnp.zeros_like(start)
    carry = (start, jnp.exp2(EXTINCT2 * start), zero, zero, zero, zero)
    return lax.fori_loop(0, last - first + 1, step, carry, unroll=unroll)


LANES = 128
UNROLL_INNER = 10
UNROLL_OUTER = 8


def inner_kernel(rank, cells, left, right, along_zy, along_x, beside, edge, layers, part, slope):
    depth, rows, _ = cells.shape
    band = edge.shape[1] // 2
    chunk = 8
    for first in range(0, depth, chunk):
        span = slice(first, first + chunk)
        sides = jnp.concatenate(
            [left[span].reshape(chunk * rows, 128), right[span].reshape(chunk * rows, 128)], 1
        )
        inner = cells[span].reshape(chunk * rows, XB)
        slope[span] = (dot(inner, along_x[...]) + dot(sides, beside[0])).reshape(chunk, rows, XB)
    nothing = jnp.zeros((1, rows, XB), cells.dtype)
    for first in range(0, depth, 2):
        low = nothing if first == 0 else cells[first - 1 : first]
        high = nothing if first + 2 == depth else cells[first + 2 : first + 3]
        stack = jnp.concatenate([low, cells[first : first + 2], high], 0)
        slope[first : first + 2] += dot(
            along_zy[...], stack.reshape(4 * rows, XB)
        ).reshape(2, rows, XB)
    edge[:, :band] = slope[:, :band]
    edge[:, band:] = slope[:, rows - band :]
    layers[0] = slope[0, band : rows - band]
    layers[1] = slope[depth - 1, band : rows - band]

    ascend = rank[0] == 0
    begin = jnp.where(ascend, 0, depth - 1)
    for row in range(band, rows - band, band):
        for lane in range(0, XB, LANES):
            at = (slice(row, row + band), slice(lane, lane + LANES))
            cell = lambda z: scaled(cells[(z, *at)])
            total, _, *sums = march(
                cell, lambda z: slope[(z, *at)], ascend, 1, depth - 2, cell(begin), UNROLL_INNER
            )
            total = total + cell(depth - 1 - begin)
            to = (slice(row - band, row), at[1])
            for n, color in enumerate(colors_of(*sums)):
                part[(n, *to)] = color
            part[(3, *to)] = jnp.exp2(EXTINCT2 * total)


def outer_kernel(
    rank, low_rows, high_rows, low_cells, high_cells, edge, layers, part,
    below, above, front, back, *rest
):
    outs, done = rest[:-1], rest[-1]
    depth, band, _ = low_rows.shape
    quarters = len(outs)
    rows = low_cells.shape[1]
    ascend = rank[0] == 0
    me = lax.axis_index("depth")
    edge[:, :1, :] -= 12.0 * front[...].astype(jnp.float32)
    edge[:, 2 * band - 1 :, :] += 12.0 * back[...].astype(jnp.float32)
    for n, sign, halo in ((0, -15.0, below), (depth - 1, 15.0, above)):
        edge[n, :band] += sign * halo[0, :band].astype(jnp.float32)
        edge[n, band:] += sign * halo[0, rows - band :].astype(jnp.float32)

    def put(g, at, colors, through):
        done[(g, 0, *at)] = encode(colors[0]) + (encode(colors[1]) << 16)
        done[(g, 1, *at)] = encode(colors[2]) + (encode(through) << 16)

    for g, cells, row in ((0, low_rows, 0), (quarters - 1, high_rows, band)):
        for lane in range(0, XB, LANES):
            lanes = slice(lane, lane + LANES)
            cell = lambda z: scaled(cells[z, :, lanes])
            slope = lambda z: edge[z, row : row + band, lanes]
            zero = jnp.zeros((band, LANES), jnp.float32)
            _, through, *sums = march(cell, slope, ascend, 0, depth - 1, zero, UNROLL_OUTER)
            put(g, (slice(0, band), lanes), colors_of(*sums), through)
    for g in range(1, quarters - 1):
        for lane in range(0, XB, LANES):
            lanes = slice(lane, lane + LANES)
            here = slice(g * band, (g + 1) * band)
            at = slice((g - 1) * band, g * band)
            through = part[3, at, lanes]
            density = [scaled(c[0, here, lanes]) for c in (low_cells, high_cells)]
            halo = [c[0, here, lanes].astype(jnp.float32) for c in (below, above)]
            sums = None
            for n, sign in ((0, -15.0), (1, 15.0)):
                clear = jnp.exp2(EXTINCT2 * density[n])
                nearest = ascend if n == 0 else jnp.logical_not(ascend)
                weight = jnp.where(
                    nearest, 1.0 - clear, through / clear - through
                )
                terms = shade(layers[n, at, lanes] + sign * halo[n], density[n], weight)
                sums = terms if sums is None else [s + t for s, t in zip(sums, terms)]
            colors = [c + part[n, at, lanes] for n, c in enumerate(colors_of(*sums))]
            put(g, (slice(0, band), lanes), colors, through)
    for k in range(quarters):
        outs[k][...] = done[lax.rem(me + k, quarters)]


def render_inner(depth_rank, density, quarters):
    depth, rows, columns = density.shape
    blocks, band = columns // XB, rows // quarters
    middle = rows - 2 * band
    in_specs = [
        pl.BlockSpec(memory_space=pltpu.SMEM),
        pl.BlockSpec((depth, rows, XB), lambda i: (0, 0, i)),
        pl.BlockSpec((depth, rows, 128), lambda i: (0, 0, jnp.maximum(2 * i - 1, 0))),
        pl.BlockSpec((depth, rows, 128), lambda i: (0, 0, jnp.minimum(2 * i + 2, 2 * blocks - 1))),
        pl.BlockSpec((2 * rows, 4 * rows), lambda i: (0, 0)),
        pl.BlockSpec((XB, XB), lambda i: (0, 0)),
        pl.BlockSpec(
            (1, XB, XB),
            lambda i: (jnp.where(i == 0, 0, jnp.where(i == blocks - 1, 2, 1)), 0, 0),
        ),
    ]
    shapes = [(depth, 2 * band), (2, middle), (4, middle)]
    cells = depth * rows * columns
    return pl.pallas_call(
        inner_kernel,
        grid=(blocks,),
        in_specs=in_specs,
        out_specs=[pl.BlockSpec((a, b, XB), lambda i: (0, 0, i)) for a, b in shapes],
        out_shape=[jax.ShapeDtypeStruct((a, b, columns), jnp.float32) for a, b in shapes],
        scratch_shapes=[pltpu.VMEM((depth, rows, XB), jnp.float32)],
        compiler_params=pltpu.CompilerParams(vmem_limit_bytes=VMEM_INNER),
        cost_estimate=pl.CostEstimate(
            flops=1000 * cells, bytes_accessed=8 * cells, transcendentals=5 * cells
        ),
        name="inner",
    )(depth_rank, density, density, density, *difference_matrices(rows))


VMEM_INNER = 56 * 2**20
VMEM_OUTER = 60 * 2**20


def render_outer(depth_rank, density, inner, below, above, front, back, quarters):
    depth, rows, columns = density.shape
    blocks, band = columns // XB, rows // quarters
    middle = rows - 2 * band
    full = lambda a, b: pl.BlockSpec((a, b, XB), lambda i: (0, 0, i))
    in_specs = [
        pl.BlockSpec(memory_space=pltpu.SMEM),
        full(depth, band),
        pl.BlockSpec((depth, band, XB), lambda i: (0, quarters - 1, i)),
        full(1, rows),
        pl.BlockSpec((1, rows, XB), lambda i: (depth - 1, 0, i)),
        full(depth, 2 * band),
        full(2, middle),
        full(4, middle),
        full(1, rows),
        full(1, rows),
        full(depth, 1),
        full(depth, 1),
    ]
    return pl.pallas_call(
        outer_kernel,
        grid=(blocks,),
        in_specs=in_specs,
        out_specs=[full(2, band)] * quarters,
        out_shape=[jax.ShapeDtypeStruct((2, band, columns), jnp.int32)] * quarters,
        scratch_shapes=[pltpu.VMEM((quarters, 2, band, XB), jnp.int32)],
        compiler_params=pltpu.CompilerParams(vmem_limit_bytes=VMEM_OUTER),
        name="outer",
    )(depth_rank, density, density, density, density, *inner, below, above, front, back)


def decode(words):
    low = (words & 65535).astype(jnp.float32) * (1.0 / CODE)
    high = ((words >> 16) & 65535).astype(jnp.float32) * (1.0 / CODE)
    return low, high


def tile_bytes(value):
    code = jnp.floor(value * CODE + 0.5)
    high = jnp.floor(code * (1.0 / 256.0))
    return high.astype(jnp.bfloat16), (code - 256.0 * high).astype(jnp.bfloat16)


def gather_kernel(rank, home, *refs):
    bricks, out = refs[:-1], refs[-1]
    members = len(bricks)
    _, band, columns = bricks[0].shape
    across = columns // PIECE
    count = band * across
    ascend = rank[0] == 0
    me = lax.axis_index("depth")
    places = []
    for k in range(members):
        index = lax.rem(me - k + members, members)
        places.append(jnp.where(ascend, index, members - 1 - index))

    piece = lax.broadcasted_iota(jnp.int32, (count, count), 0)
    column = lax.broadcasted_iota(jnp.int32, (count, count), 1)
    homes = home[...]
    regroup = (piece == lax.rem(column, band) * across + column // band).astype(jnp.bfloat16)
    named = (piece == (homes // count)).astype(jnp.bfloat16)
    earlier = dot(named, (piece < column).astype(jnp.bfloat16))
    slots = (homes % count + 1).astype(jnp.float32)
    label = jnp.zeros((count, 128), jnp.int32)
    lane = lax.broadcasted_iota(jnp.int32, (count, 128), 1)
    routes = []
    for e in range(2):
        chosen = named.astype(jnp.float32) * (earlier == float(e)).astype(jnp.float32)
        here = jnp.sum(chosen * slots, axis=1, keepdims=True).astype(jnp.int32)
        label = label + jnp.where(lane == e, here, 0)
        routes.append(dot(chosen.astype(jnp.bfloat16), regroup).astype(jnp.bfloat16))
    out[:, 2 * PAYLOAD :] = label

    planes = [[], [], []]
    for c in range(across):
        part = slice(c * PIECE, (c + 1) * PIECE)
        colors, clears = [], []
        for brick in bricks:
            first, second = decode(brick[0, :, part])
            third, clear = decode(brick[1, :, part])
            colors.append((first, second, third))
            clears.append(clear)
        total = clears[0]
        for clear in clears[1:]:
            total = total * clear
        done = [total * b for b in BACKDROP]
        for k in range(members):
            ahead = None
            for other in range(members):
                if other != k:
                    factor = jnp.where(places[other] < places[k], clears[other], 1.0)
                    ahead = factor if ahead is None else ahead * factor
            done = [d + ahead * color for d, color in zip(done, colors[k])]
        for channel in range(3):
            planes[channel].append(tile_bytes(done[channel]))
    for channel in range(3):
        high = jnp.concatenate([p[0] for p in planes[channel]], 0)
        low = jnp.concatenate([p[1] for p in planes[channel]], 0)
        for e in range(2):
            code = (256.0 * dot(routes[e], high) + dot(routes[e], low)).astype(jnp.int32)
            words = code[:, :HALF] + (code[:, HALF:] << 16)
            at = e * PAYLOAD + channel * HALF
            out[:, at : at + HALF] = words


def gather(depth_rank, piece_home, bricks):
    _, band, columns = bricks[0].shape
    count = piece_home.shape[0]
    vmem = pl.BlockSpec(memory_space=pltpu.VMEM)
    return pl.pallas_call(
        gather_kernel,
        in_specs=[pl.BlockSpec(memory_space=pltpu.SMEM)] + [vmem] * (1 + len(bricks)),
        out_specs=vmem,
        out_shape=jax.ShapeDtypeStruct((count, ROW_WORDS), jnp.int32),
        compiler_params=pltpu.CompilerParams(vmem_limit_bytes=24 * 2**20),
        name="gather",
    )(depth_rank, piece_home.reshape(1, count), *bricks)


def place_kernel(arrived, out):
    count = arrived.shape[0]
    slot = lax.broadcasted_iota(jnp.int32, (count, count), 1)
    choices = [
        (arrived[:, 2 * PAYLOAD + e : 2 * PAYLOAD + e + 1] == slot + 1).astype(jnp.bfloat16)
        for e in range(2)
    ]
    choice = jnp.concatenate(choices, 0)

    def plane(words, shift):
        return ((words >> shift) & 255).astype(jnp.float32).astype(jnp.bfloat16)

    def put(planes):
        return lax.dot_general(
            choice, planes, (((0,), (0,)), ((), ())), preferred_element_type=jnp.float32
        )

    for channel in range(3):
        at = channel * HALF
        words = jnp.concatenate(
            [arrived[:, e * PAYLOAD + at : e * PAYLOAD + at + HALF] for e in range(2)], 0
        )
        for half in range(2):
            code = 256.0 * put(plane(words, 16 * half + 8)) + put(plane(words, 16 * half))
            out[channel, 0, :, half * HALF : (half + 1) * HALF] = code * (1.0 / CODE)


def place(arrived):
    count = arrived.shape[0]
    vmem = pl.BlockSpec(memory_space=pltpu.VMEM)
    return pl.pallas_call(
        place_kernel,
        in_specs=[vmem],
        out_specs=vmem,
        out_shape=jax.ShapeDtypeStruct((3, 1, count, PIECE), jnp.float32),
        compiler_params=pltpu.CompilerParams(vmem_limit_bytes=24 * 2**20),
        name="place",
    )(arrived)


def neighbors(shard, axis, dim):
    peers, length = lax.axis_size(axis), shard.shape[dim]
    up = [(i, i + 1) for i in range(peers - 1)]
    last = lax.slice_in_dim(shard, length - 1, length, axis=dim)
    first = lax.slice_in_dim(shard, 0, 1, axis=dim)
    return lax.ppermute(last, axis, up), lax.ppermute(first, axis, [(b, a) for a, b in up])


def on_device(density, depth_rank, piece_home):
    members = lax.axis_size("depth")
    below, above = neighbors(density, "depth", 0)
    front, back = neighbors(density, "tile", 1)
    inner = render_inner(depth_rank, density, members)
    parts = render_outer(depth_rank, density, inner, below, above, front, back, members)
    bricks = [parts[0]]
    for k in range(1, members):
        ring = [(i, (i + k) % members) for i in range(members)]
        bricks.append(lax.ppermute(parts[k], "depth", ring))
    outbox = gather(depth_rank, piece_home, bricks)
    arrived = lax.all_to_all(outbox, "tile", split_axis=0, concat_axis=0, tiled=True)
    return place(arrived)


def solution(mesh):
    in_specs = (P("depth", "tile", None), P(), P("tile"))
    out_specs = P(None, "depth", "tile", None)
    return jax.shard_map(
        on_device, mesh=mesh, in_specs=in_specs, out_specs=out_specs, check_vma=False
    )
```

```python
import functools
import math

import jax
import jax.numpy as jnp
import numpy as np
from jax import lax
from jax.experimental import pallas as pl
from jax.experimental.pallas import tpu as pltpu
from jax.sharding import PartitionSpec as P

EXTINCT = 0.5
BACKDROP = (0.08, 0.1, 0.14)
CODE = 65535.0

XB = 256
PIECE = 512
HALF = PIECE // 2
PAYLOAD = 3 * HALF
ROW_WORDS = 2 * PAYLOAD + 128


def cosine_polynomial(degree):
    limit = (0.85 * math.log(0.01) + math.pi / 2) ** 2 * 1.0005
    nodes = np.cos(np.pi * (np.arange(4000) + 0.5) / 4000)
    points = (nodes + 1) * limit / 2
    fit = np.polynomial.chebyshev.Chebyshev.fit(
        points, np.cos(np.sqrt(points)), degree, domain=[0, limit]
    )
    return [float(c) for c in fit.convert(kind=np.polynomial.Polynomial).coef]


COS = cosine_polynomial(4)
SHIFT = math.exp(math.pi / 1.7)
OFFSET = 0.01 * SHIFT
EXTINCT2 = -0.5 * math.log2(math.e) / SHIFT
NEAR = SHIFT * math.exp(-3.0)
FAR = SHIFT * math.exp(-2.5)
MONIC = [COS[i] / COS[4] / 0.85 ** (8 - 2 * i) for i in range(4)]
COSINE_SCALE = (COS[4] * 0.85**8) ** 2


def difference_matrices(along_zy, along_x, beside):
    def bands(ref, shape, pairs):
        row = lax.broadcasted_iota(jnp.int32, shape, 0)
        column = lax.broadcasted_iota(jnp.int32, shape, 1)
        total = jnp.zeros(shape, jnp.float32)
        for value, where in pairs:
            total = jnp.where(where(row, column), value, total)
        ref[...] = total.astype(ref.dtype)

    bands(
        along_x,
        (XB, XB),
        ((16.0, lambda i, j: i == j + 1), (-16.0, lambda i, j: i + 1 == j)),
    )
    left = (-16.0, lambda i, j: (i == 127) & (j == 0))
    right = (16.0, lambda i, j: (i == 128) & (j == XB - 1))
    for n, pairs in enumerate(((right,), (left, right), (left,))):
        bands(beside.at[n], (XB, XB), pairs)
    rows = along_zy.shape[0] // 2
    inside = lambda i: lax.rem(i, rows)
    bands(
        along_zy,
        (2 * rows, 4 * rows),
        (
            (15.0, lambda i, j: j == i + 2 * rows),
            (-15.0, lambda i, j: j == i),
            (12.0, lambda i, j: (j == i + rows + 1) & (inside(i) < rows - 1)),
            (-12.0, lambda i, j: (j == i + rows - 1) & (inside(i) > 0)),
        ),
    )


def dot(a, b):
    return jnp.dot(a, b, preferred_element_type=jnp.float32)


def encode(value):
    return (value * CODE + 0.5).astype(jnp.int32)


def shade(facing_sum, density, weight):
    weight = weight * (jnp.tanh(0.12 * facing_sum) + 0.675 / 0.325)
    logged = jnp.log(density + OFFSET)
    square = logged * logged
    c0, c1, c2, c3 = MONIC
    cosine = (((square + c3) * square + c2) * square + c1) * square + c0
    near = pltpu.reciprocal(density + (OFFSET + NEAR))
    far = pltpu.reciprocal(density + (OFFSET + FAR))
    return weight, weight * near, weight * (cosine * cosine), weight * far


def colors_of(plain, sum0, sum1, sum2):
    plain = 0.325 * plain
    return plain - (0.325 * NEAR) * sum0, plain - (0.325 * COSINE_SCALE) * sum1, (0.325 * FAR) * sum2


def scaled(cells):
    return SHIFT * cells.astype(jnp.float32)


def advance(z, cell, slope, carry):
    total, clear, *sums = carry
    density = cell(z)
    total = total + density
    after = jnp.exp2(EXTINCT2 * total)
    terms = shade(slope(z), density, clear - after)
    return (total, after, *(s + t for s, t in zip(sums, terms)))


def behind_first(start):
    zero = jnp.zeros_like(start)
    return start, jnp.exp2(EXTINCT2 * start), zero, zero, zero, zero


def march(cell, slope, ascend, first, last, start, unroll):
    def step(i, carry):
        return advance(jnp.where(ascend, first + i, last - i), cell, slope, carry)

    return lax.fori_loop(0, last - first + 1, step, behind_first(start), unroll=unroll)


SEGMENT = 8
LANES = 128
UNROLL_OUTER = 30


def inner_kernel(
    rank, density, cells, edge, layers, part, slope0, slope1, along_zy, along_x, beside, arrivals
):
    slopes = (slope0, slope1)
    depth, rows, columns = cells.shape
    band = edge.shape[1] // 2
    blocks = columns // XB
    ascend = rank[0] == 0
    begin = jnp.where(ascend, 0, depth - 1)
    tiles = [
        (row, lane) for row in range(0, rows - 2 * band, band) for lane in range(0, XB, LANES)
    ]
    chunk = SEGMENT

    def arrival(block):
        lanes = pl.ds(pl.multiple_of(block * XB, XB), XB)
        return pltpu.make_async_copy(
            density.at[:, :, lanes], cells.at[:, :, lanes], arrivals.at[block]
        )

    def differences(block, n, slope):
        lanes = pl.ds(pl.multiple_of(block * XB, XB), XB)
        left = pl.ds(pl.multiple_of(jnp.maximum(block * XB - 128, 0), 128), 128)
        right = pl.ds(pl.multiple_of(jnp.minimum(block * XB + XB, columns - 128), 128), 128)
        kind = jnp.where(block == 0, 0, jnp.where(block == blocks - 1, 2, 1))
        span = slice(n * chunk, (n + 1) * chunk)
        flat = lambda at: cells[span, :, at].reshape(chunk * rows, -1)
        sides = jnp.concatenate([flat(left), flat(right)], 1)
        across = dot(flat(lanes), along_x[...]) + dot(sides, beside[kind])
        nothing = jnp.zeros((1, rows, XB), cells.dtype)
        found = []
        for pair in range(0, chunk, 2):
            z = n * chunk + pair
            low = nothing if z == 0 else cells[z - 1 : z, :, lanes]
            high = nothing if z + 2 == depth else cells[z + 2 : z + 3, :, lanes]
            stack = jnp.concatenate([low, cells[z : z + 2, :, lanes], high], 0)
            both = across[pair * rows : (pair + 2) * rows] + dot(
                along_zy[...], stack.reshape(4 * rows, XB)
            )
            found.append((z, both.reshape(2, rows, XB)))
        return found

    def keep(block, found, slope):
        lanes = pl.ds(pl.multiple_of(block * XB, XB), XB)
        for z, both in found:
            edge[z : z + 2, :band, lanes] = both[:, :band]
            edge[z : z + 2, band:, lanes] = both[:, rows - band :]
            slope[z : z + 2] = both[:, band : rows - band]
            if z == 0:
                layers[0, :, lanes] = both[0, band : rows - band]
            if z + 2 == depth:
                layers[1, :, lanes] = both[1, band : rows - band]

    def rays(block, slope):
        for row, lane in tiles:
            lanes = pl.ds(pl.multiple_of(block * XB + lane, 128), LANES)
            here = slice(row, row + band)
            cell = lambda z: scaled(cells[z, band + row : 2 * band + row, lanes])
            facing = lambda z: slope[z, here, lane : lane + LANES]
            carry = behind_first(cell(begin))
            for i in range(1, depth - 1):
                carry = advance(jnp.where(ascend, i, depth - 1 - i), cell, facing, carry)
                if i < depth - 2:
                    yield
            total, _, *sums = carry
            total = total + cell(depth - 1 - begin)
            for n, color in enumerate(colors_of(*sums)):
                part[n, here, lanes] = color
            part[3, here, lanes] = jnp.exp2(EXTINCT2 * total)
            yield

    def both(ahead, behind, parity):
        cells_left = iter(()) if behind is None else rays(behind, slopes[1 - parity])
        segments = depth // chunk
        steps = (depth - 2) * len(tiles)
        for n in range(segments):
            found = [] if ahead is None else differences(ahead, n, slopes[parity])
            for _ in range(steps * (n + 1) // segments - steps * n // segments):
                next(cells_left, None)
            keep(ahead, found, slopes[parity]) if found else None

    for block in range(blocks):
        arrival(block).start()
    difference_matrices(along_zy, along_x, beside)
    arrival(0).wait()
    arrival(1).wait()
    both(0, None, 0)

    @pl.loop(0, blocks // 2 - 1)
    def _(pair):
        arrival(2 * pair + 2).wait()
        both(2 * pair + 1, 2 * pair, 1)
        arrival(2 * pair + 3).wait()
        both(2 * pair + 2, 2 * pair + 1, 0)

    both(blocks - 1, blocks - 2, 1)
    both(None, blocks - 1, 0)


def outer_kernel(
    rank, cells, edge, layers, part, below, above, front, back, *rest
):
    outs, done, ends = rest[:-2], rest[-2], rest[-1]
    depth, rows, columns = cells.shape
    quarters = len(outs)
    band = rows // quarters
    ascend = rank[0] == 0
    me = lax.axis_index("depth")
    first8 = lax.broadcasted_iota(jnp.int32, (8, LANES), 0)

    def put(g, lanes, colors, through):
        done[g, 0, :, lanes] = encode(colors[0]) + (encode(colors[1]) << 16)
        done[g, 1, :, lanes] = encode(colors[2]) + (encode(through) << 16)

    @pl.loop(0, columns // LANES)
    def _(column):
        lanes = pl.ds(pl.multiple_of(column * LANES, LANES), LANES)
        for n, halo, factor in ((0, front, -12.0), (1, back, 12.0)):
            lines = factor * halo[:, lanes].astype(jnp.float32)
            for z in range(depth):
                ends[n, z] = jnp.where(first8 == 7 * n, lines[z : z + 1], 0.0)
        for g in range(quarters):
            here = slice(g * band, (g + 1) * band)
            cell = lambda z: scaled(cells[z, here, lanes])
            begin = jnp.where(ascend, 0, depth - 1)
            if g in (0, quarters - 1):
                at = slice(0, band) if g == 0 else slice(band, 2 * band)

                def slope(z):
                    tile = edge[z, at, lanes]
                    if g:
                        return jnp.concatenate([tile[:-8], tile[-8:] + ends[1, z]], 0)
                    return jnp.concatenate([tile[:8] + ends[0, z], tile[8:]], 0)

                total, _, *sums = march(
                    cell, slope, ascend, 1, depth - 2, cell(begin), UNROLL_OUTER
                )
                colors = colors_of(*sums)
                through = jnp.exp2(EXTINCT2 * (total + cell(depth - 1 - begin)))
                slopes = [slope(z) for z in (0, depth - 1)]
            else:
                at = slice((g - 1) * band, g * band)
                colors = [part[n, at, lanes] for n in range(3)]
                through = part[3, at, lanes]
                slopes = [layers[n, at, lanes] for n in range(2)]
            sums = None
            for n, z, sign, halo in ((0, 0, -15.0, below), (1, depth - 1, 15.0, above)):
                density = cell(z)
                clear = jnp.exp2(EXTINCT2 * density)
                nearest = ascend if n == 0 else jnp.logical_not(ascend)
                weight = jnp.where(nearest, 1.0 - clear, through / clear - through)
                facing = slopes[n] + sign * halo[0, here, lanes].astype(jnp.float32)
                terms = shade(facing, density, weight)
                sums = terms if sums is None else [s + t for s, t in zip(sums, terms)]
            put(g, lanes, [c + d for c, d in zip(colors, colors_of(*sums))], through)

    for k in range(quarters):
        outs[k][...] = done[lax.rem(me + k, quarters)]


VMEM_INNER = 24 * 2**20
VMEM_OUTER = 24 * 2**20
WHOLE = pl.BlockSpec(memory_space=pltpu.VMEM)


def render_inner(depth_rank, density, quarters):
    depth, rows, columns = density.shape
    band = rows // quarters
    middle = rows - 2 * band
    shapes = [(depth, 2 * band), (2, middle), (4, middle)]
    cells = depth * rows * columns
    return pl.pallas_call(
        inner_kernel,
        in_specs=[pl.BlockSpec(memory_space=pltpu.SMEM), pl.BlockSpec(memory_space=pltpu.HBM)],
        out_specs=[WHOLE] * 4,
        out_shape=[pltpu.VMEM(density.shape, density.dtype)]
        + [pltpu.VMEM((a, b, columns), jnp.float32) for a, b in shapes],
        scratch_shapes=[pltpu.VMEM((depth, middle, XB), jnp.float32)] * 2
        + [
            pltpu.VMEM((2 * rows, 4 * rows), density.dtype),
            pltpu.VMEM((XB, XB), density.dtype),
            pltpu.VMEM((3, XB, XB), density.dtype),
            pltpu.SemaphoreType.DMA((columns // XB,)),
        ],
        compiler_params=pltpu.CompilerParams(vmem_limit_bytes=VMEM_INNER),
        cost_estimate=pl.CostEstimate(
            flops=1000 * cells, bytes_accessed=8 * cells, transcendentals=5 * cells
        ),
        name="inner",
    )(depth_rank, pltpu.with_memory_space_constraint(density, pltpu.HBM))


def render_outer(depth_rank, inner, below, above, front, back, quarters):
    depth, rows, columns = inner[0].shape
    band = rows // quarters
    return pl.pallas_call(
        outer_kernel,
        in_specs=[pl.BlockSpec(memory_space=pltpu.SMEM)] + [WHOLE] * 8,
        out_specs=[WHOLE] * quarters,
        out_shape=[jax.ShapeDtypeStruct((2, band, columns), jnp.int32)] * quarters,
        scratch_shapes=[
            pltpu.VMEM((quarters, 2, band, columns), jnp.int32),
            pltpu.VMEM((2, depth, 8, LANES), jnp.float32),
        ],
        compiler_params=pltpu.CompilerParams(vmem_limit_bytes=VMEM_OUTER),
        name="outer",
    )(depth_rank, *inner, below, above, front, back)


def decode(words):
    low = (words & 65535).astype(jnp.float32) * (1.0 / CODE)
    high = ((words >> 16) & 65535).astype(jnp.float32) * (1.0 / CODE)
    return low, high


def tile_bytes(value):
    code = jnp.floor(value * CODE + 0.5)
    high = jnp.floor(code * (1.0 / 256.0))
    return high.astype(jnp.bfloat16), (code - 256.0 * high).astype(jnp.bfloat16)


def gather_kernel(rank, home, *refs):
    bricks, out = refs[:-1], refs[-1]
    members = len(bricks)
    _, band, columns = bricks[0].shape
    across = columns // PIECE
    count = band * across
    ascend = rank[0] == 0
    me = lax.axis_index("depth")
    places = []
    for k in range(members):
        index = lax.rem(me - k + members, members)
        places.append(jnp.where(ascend, index, members - 1 - index))

    piece = lax.broadcasted_iota(jnp.int32, (count, count), 0)
    column = lax.broadcasted_iota(jnp.int32, (count, count), 1)
    homes = home[...]
    regroup = (piece == lax.rem(column, band) * across + column // band).astype(jnp.bfloat16)
    named = (piece == (homes // count)).astype(jnp.bfloat16)
    earlier = dot(named, (piece < column).astype(jnp.bfloat16))
    slots = (homes % count + 1).astype(jnp.float32)
    label = jnp.zeros((count, 128), jnp.int32)
    lane = lax.broadcasted_iota(jnp.int32, (count, 128), 1)
    routes = []
    for e in range(2):
        chosen = named.astype(jnp.float32) * (earlier == float(e)).astype(jnp.float32)
        here = jnp.sum(chosen * slots, axis=1, keepdims=True).astype(jnp.int32)
        label = label + jnp.where(lane == e, here, 0)
        routes.append(dot(chosen.astype(jnp.bfloat16), regroup).astype(jnp.bfloat16))
    out[:, 2 * PAYLOAD :] = label

    planes = [[], [], []]
    for c in range(across):
        part = slice(c * PIECE, (c + 1) * PIECE)
        colors, clears = [], []
        for brick in bricks:
            first, second = decode(brick[0, :, part])
            third, clear = decode(brick[1, :, part])
            colors.append((first, second, third))
            clears.append(clear)
        total = clears[0]
        for clear in clears[1:]:
            total = total * clear
        done = [total * b for b in BACKDROP]
        for k in range(members):
            ahead = None
            for other in range(members):
                if other != k:
                    factor = jnp.where(places[other] < places[k], clears[other], 1.0)
                    ahead = factor if ahead is None else ahead * factor
            done = [d + ahead * color for d, color in zip(done, colors[k])]
        for channel in range(3):
            planes[channel].append(tile_bytes(done[channel]))
    for channel in range(3):
        high = jnp.concatenate([p[0] for p in planes[channel]], 0)
        low = jnp.concatenate([p[1] for p in planes[channel]], 0)
        for e in range(2):
            code = (256.0 * dot(routes[e], high) + dot(routes[e], low)).astype(jnp.int32)
            words = code[:, :HALF] + (code[:, HALF:] << 16)
            at = e * PAYLOAD + channel * HALF
            out[:, at : at + HALF] = words


def gather(depth_rank, piece_home, bricks):
    _, band, columns = bricks[0].shape
    count = piece_home.shape[0]
    vmem = pl.BlockSpec(memory_space=pltpu.VMEM)
    return pl.pallas_call(
        gather_kernel,
        in_specs=[pl.BlockSpec(memory_space=pltpu.SMEM)] + [vmem] * (1 + len(bricks)),
        out_specs=vmem,
        out_shape=jax.ShapeDtypeStruct((count, ROW_WORDS), jnp.int32),
        compiler_params=pltpu.CompilerParams(vmem_limit_bytes=24 * 2**20),
        name="gather",
    )(depth_rank, piece_home.reshape(1, count), *bricks)


def place_kernel(arrived, out):
    count = arrived.shape[0]
    slot = lax.broadcasted_iota(jnp.int32, (count, count), 1)
    choices = [
        (arrived[:, 2 * PAYLOAD + e : 2 * PAYLOAD + e + 1] == slot + 1).astype(jnp.bfloat16)
        for e in range(2)
    ]
    choice = jnp.concatenate(choices, 0)

    def plane(words, shift):
        return ((words >> shift) & 255).astype(jnp.float32).astype(jnp.bfloat16)

    def put(planes):
        return lax.dot_general(
            choice, planes, (((0,), (0,)), ((), ())), preferred_element_type=jnp.float32
        )

    for channel in range(3):
        at = channel * HALF
        words = jnp.concatenate(
            [arrived[:, e * PAYLOAD + at : e * PAYLOAD + at + HALF] for e in range(2)], 0
        )
        for half in range(2):
            code = 256.0 * put(plane(words, 16 * half + 8)) + put(plane(words, 16 * half))
            out[channel, 0, :, half * HALF : (half + 1) * HALF] = code * (1.0 / CODE)


def place(arrived):
    count = arrived.shape[0]
    vmem = pl.BlockSpec(memory_space=pltpu.VMEM)
    return pl.pallas_call(
        place_kernel,
        in_specs=[vmem],
        out_specs=vmem,
        out_shape=jax.ShapeDtypeStruct((3, 1, count, PIECE), jnp.float32),
        compiler_params=pltpu.CompilerParams(vmem_limit_bytes=24 * 2**20),
        name="place",
    )(arrived)


def from_neighbors(first, last, axis):
    peers = lax.axis_size(axis)
    up = [(i, i + 1) for i in range(peers - 1)]
    return lax.ppermute(last, axis, up), lax.ppermute(first, axis, [(b, a) for a, b in up])


def on_device(density, depth_rank, piece_home):
    members = lax.axis_size("depth")
    below, above = from_neighbors(density[:1], density[-1:], "depth")
    front, back = from_neighbors(density[:, 0], density[:, -1], "tile")
    inner = render_inner(depth_rank, density, members)
    parts = render_outer(depth_rank, inner, below, above, front, back, members)
    bricks = [parts[0]]
    for k in range(1, members):
        ring = [(i, (i + k) % members) for i in range(members)]
        bricks.append(lax.ppermute(parts[k], "depth", ring))
    outbox = gather(depth_rank, piece_home, bricks)
    arrived = lax.all_to_all(outbox, "tile", split_axis=0, concat_axis=0, tiled=True)
    return place(arrived)


def solution(mesh):
    in_specs = (P("depth", "tile", None), P(), P("tile"))
    out_specs = P(None, "depth", "tile", None)
    return jax.shard_map(
        on_device, mesh=mesh, in_specs=in_specs, out_specs=out_specs, check_vma=False
    )
```

```python
import functools
import math

import jax
import jax.numpy as jnp
import numpy as np
from jax import lax
from jax.experimental import pallas as pl
from jax.experimental.pallas import tpu as pltpu
from jax.sharding import PartitionSpec as P

EXTINCT = 0.5
BACKDROP = (0.08, 0.1, 0.14)
CODE = 65535.0

XB = 256
PIECE = 512
HALF = PIECE // 2
PAYLOAD = 3 * HALF
ROW_WORDS = 2 * PAYLOAD + 128


def cosine_polynomial(degree):
    limit = (0.85 * math.log(0.01) + math.pi / 2) ** 2 * 1.0005
    nodes = np.cos(np.pi * (np.arange(4000) + 0.5) / 4000)
    points = (nodes + 1) * limit / 2
    fit = np.polynomial.chebyshev.Chebyshev.fit(
        points, np.cos(np.sqrt(points)), degree, domain=[0, limit]
    )
    return [float(c) for c in fit.convert(kind=np.polynomial.Polynomial).coef]


COS = cosine_polynomial(4)
SHIFT = math.exp(math.pi / 1.7)
OFFSET = 0.01 * SHIFT
EXTINCT2 = -0.5 * math.log2(math.e) / SHIFT
NEAR = SHIFT * math.exp(-3.0)
FAR = SHIFT * math.exp(-2.5)
MONIC = [COS[i] / COS[4] / 0.85 ** (8 - 2 * i) for i in range(4)]
COSINE_SCALE = (COS[4] * 0.85**8) ** 2


def difference_matrices(along_zy, along_x, beside):
    def bands(ref, shape, pairs):
        row = lax.broadcasted_iota(jnp.int32, shape, 0)
        column = lax.broadcasted_iota(jnp.int32, shape, 1)
        total = jnp.zeros(shape, jnp.float32)
        for value, where in pairs:
            total = jnp.where(where(row, column), value, total)
        ref[...] = total.astype(ref.dtype)

    bands(
        along_x,
        (XB, XB),
        ((16.0, lambda i, j: i == j + 1), (-16.0, lambda i, j: i + 1 == j)),
    )
    left = (-16.0, lambda i, j: (i == 127) & (j == 0))
    right = (16.0, lambda i, j: (i == 128) & (j == XB - 1))
    for n, pairs in enumerate(((right,), (left, right), (left,))):
        bands(beside.at[n], (XB, XB), pairs)
    rows = along_zy.shape[0] // 2
    inside = lambda i: lax.rem(i, rows)
    bands(
        along_zy,
        (2 * rows, 4 * rows),
        (
            (15.0, lambda i, j: j == i + 2 * rows),
            (-15.0, lambda i, j: j == i),
            (12.0, lambda i, j: (j == i + rows + 1) & (inside(i) < rows - 1)),
            (-12.0, lambda i, j: (j == i + rows - 1) & (inside(i) > 0)),
        ),
    )


def dot(a, b):
    return jnp.dot(a, b, preferred_element_type=jnp.float32)


def encode(value):
    return (value * CODE + 0.5).astype(jnp.int32)


def shade(facing_sum, density, weight):
    weight = weight * (jnp.tanh(0.12 * facing_sum) + 0.675 / 0.325)
    logged = jnp.log(density + OFFSET)
    square = logged * logged
    c0, c1, c2, c3 = MONIC
    cosine = (((square + c3) * square + c2) * square + c1) * square + c0
    near = pltpu.reciprocal(density + (OFFSET + NEAR))
    far = pltpu.reciprocal(density + (OFFSET + FAR))
    return weight, weight * near, weight * (cosine * cosine), weight * far


def colors_of(plain, sum0, sum1, sum2):
    plain = 0.325 * plain
    return plain - (0.325 * NEAR) * sum0, plain - (0.325 * COSINE_SCALE) * sum1, (0.325 * FAR) * sum2


def scaled(cells):
    return SHIFT * cells.astype(jnp.float32)


def advance(z, cell, slope, carry):
    total, clear, *sums = carry
    density = cell(z)
    total = total + density
    after = jnp.exp2(EXTINCT2 * total)
    terms = shade(slope(z), density, clear - after)
    return (total, after, *(s + t for s, t in zip(sums, terms)))


def behind_first(start):
    zero = jnp.zeros_like(start)
    return start, jnp.exp2(EXTINCT2 * start), zero, zero, zero, zero


def march(cell, slope, ascend, first, last, start, unroll):
    def step(i, carry):
        return advance(jnp.where(ascend, first + i, last - i), cell, slope, carry)

    return lax.fori_loop(0, last - first + 1, step, behind_first(start), unroll=unroll)


SEGMENT = 8
LANES = 128
UNROLL_OUTER = 30


def inner_kernel(
    rank, density, cells, edge, layers, part, slope0, slope1, along_zy, along_x, beside, arrivals
):
    slopes = (slope0, slope1)
    depth, rows, columns = cells.shape
    band = edge.shape[1] // 2
    blocks = columns // XB
    ascend = rank[0] == 0
    begin = jnp.where(ascend, 0, depth - 1)
    tiles = [
        (row, lane) for row in range(0, rows - 2 * band, band) for lane in range(0, XB, LANES)
    ]
    chunk = SEGMENT

    def arrival(block):
        lanes = pl.ds(pl.multiple_of(block * XB, XB), XB)
        return pltpu.make_async_copy(
            density.at[:, :, lanes], cells.at[:, :, lanes], arrivals.at[block]
        )

    def differences(block, n, slope):
        lanes = pl.ds(pl.multiple_of(block * XB, XB), XB)
        left = pl.ds(pl.multiple_of(jnp.maximum(block * XB - 128, 0), 128), 128)
        right = pl.ds(pl.multiple_of(jnp.minimum(block * XB + XB, columns - 128), 128), 128)
        kind = jnp.where(block == 0, 0, jnp.where(block == blocks - 1, 2, 1))
        span = slice(n * chunk, (n + 1) * chunk)
        flat = lambda at: cells[span, :, at].reshape(chunk * rows, -1)
        sides = jnp.concatenate([flat(left), flat(right)], 1)
        across = dot(flat(lanes), along_x[...]) + dot(sides, beside[kind])
        nothing = jnp.zeros((1, rows, XB), cells.dtype)
        found = []
        for pair in range(0, chunk, 2):
            z = n * chunk + pair
            low = nothing if z == 0 else cells[z - 1 : z, :, lanes]
            high = nothing if z + 2 == depth else cells[z + 2 : z + 3, :, lanes]
            stack = jnp.concatenate([low, cells[z : z + 2, :, lanes], high], 0)
            both = across[pair * rows : (pair + 2) * rows] + dot(
                along_zy[...], stack.reshape(4 * rows, XB)
            )
            found.append((z, both.reshape(2, rows, XB)))
        return found

    def keep(block, found, slope):
        lanes = pl.ds(pl.multiple_of(block * XB, XB), XB)
        for z, both in found:
            edge[z : z + 2, :band, lanes] = both[:, :band]
            edge[z : z + 2, band:, lanes] = both[:, rows - band :]
            slope[z : z + 2] = both[:, band : rows - band]
            if z == 0:
                layers[0, :, lanes] = both[0, band : rows - band]
            if z + 2 == depth:
                layers[1, :, lanes] = both[1, band : rows - band]

    def rays(block, slope):
        for row, lane in tiles:
            lanes = pl.ds(pl.multiple_of(block * XB + lane, 128), LANES)
            here = slice(row, row + band)
            cell = lambda z: scaled(cells[z, band + row : 2 * band + row, lanes])
            facing = lambda z: slope[z, here, lane : lane + LANES]
            carry = behind_first(cell(begin))
            for i in range(1, depth - 1):
                carry = advance(jnp.where(ascend, i, depth - 1 - i), cell, facing, carry)
                if i < depth - 2:
                    yield
            total, _, *sums = carry
            total = total + cell(depth - 1 - begin)
            for n, color in enumerate(colors_of(*sums)):
                part[n, here, lanes] = color
            part[3, here, lanes] = jnp.exp2(EXTINCT2 * total)
            yield

    def both(ahead, behind, parity):
        cells_left = iter(()) if behind is None else rays(behind, slopes[1 - parity])
        segments = depth // chunk
        steps = (depth - 2) * len(tiles)
        for n in range(segments):
            found = [] if ahead is None else differences(ahead, n, slopes[parity])
            for _ in range(steps * (n + 1) // segments - steps * n // segments):
                next(cells_left, None)
            keep(ahead, found, slopes[parity]) if found else None

    for block in range(blocks):
        arrival(block).start()
    difference_matrices(along_zy, along_x, beside)
    arrival(0).wait()
    arrival(1).wait()
    both(0, None, 0)

    @pl.loop(0, blocks // 2 - 1)
    def _(pair):
        arrival(2 * pair + 2).wait()
        both(2 * pair + 1, 2 * pair, 1)
        arrival(2 * pair + 3).wait()
        both(2 * pair + 2, 2 * pair + 1, 0)

    both(blocks - 1, blocks - 2, 1)
    both(None, blocks - 1, 0)


def outer_kernel(k, rank, cells, edge, layers, part, below, above, front, back, out, ends):
    depth, rows, columns = cells.shape
    _, band, _ = out.shape
    quarters = rows // band
    ascend = rank[0] == 0
    band_index = lax.rem(lax.axis_index("depth") + k, quarters)
    here = pl.ds(pl.multiple_of(band_index * band, band), band)
    begin = jnp.where(ascend, 0, depth - 1)
    first8 = lax.broadcasted_iota(jnp.int32, (8, LANES), 0)

    def finish(lanes, cell, slopes, colors, through):
        sums = None
        for n, z, sign, halo in ((0, 0, -15.0, below), (1, depth - 1, 15.0, above)):
            density = cell(z)
            clear = jnp.exp2(EXTINCT2 * density)
            nearest = ascend if n == 0 else jnp.logical_not(ascend)
            weight = jnp.where(nearest, 1.0 - clear, through / clear - through)
            facing = slopes[n] + sign * halo[0, here, lanes].astype(jnp.float32)
            terms = shade(facing, density, weight)
            sums = terms if sums is None else [s + t for s, t in zip(sums, terms)]
        done = [c + d for c, d in zip(colors, colors_of(*sums))]
        out[0, :, lanes] = encode(done[0]) + (encode(done[1]) << 16)
        out[1, :, lanes] = encode(done[2]) + (encode(through) << 16)

    def outermost(last):
        at = slice(band, 2 * band) if last else slice(0, band)
        halo, factor, line = (back, 12.0, 7) if last else (front, -12.0, 0)

        @pl.loop(0, columns // LANES)
        def _(column):
            lanes = pl.ds(pl.multiple_of(column * LANES, LANES), LANES)
            cell = lambda z: scaled(cells[z, here, lanes])
            lines = factor * halo[:, lanes].astype(jnp.float32)
            for z in range(depth):
                ends[z] = jnp.where(first8 == line, lines[z : z + 1], 0.0)

            def slope(z):
                tile = edge[z, at, lanes]
                if last:
                    return jnp.concatenate([tile[:-8], tile[-8:] + ends[z]], 0)
                return jnp.concatenate([tile[:8] + ends[z], tile[8:]], 0)

            total, _, *sums = march(
                cell, slope, ascend, 1, depth - 2, cell(begin), UNROLL_OUTER
            )
            through = jnp.exp2(EXTINCT2 * (total + cell(depth - 1 - begin)))
            slopes = [slope(z) for z in (0, depth - 1)]
            finish(lanes, cell, slopes, colors_of(*sums), through)

    @pl.when(band_index == 0)
    def _():
        outermost(False)

    @pl.when(band_index == quarters - 1)
    def _():
        outermost(True)

    @pl.when(jnp.logical_and(band_index > 0, band_index < quarters - 1))
    def _():
        at = pl.ds(pl.multiple_of((band_index - 1) * band, band), band)

        @pl.loop(0, columns // LANES)
        def _(column):
            lanes = pl.ds(pl.multiple_of(column * LANES, LANES), LANES)
            cell = lambda z: scaled(cells[z, here, lanes])
            colors = [part[n, at, lanes] for n in range(3)]
            slopes = [layers[n, at, lanes] for n in range(2)]
            finish(lanes, cell, slopes, colors, part[3, at, lanes])


VMEM_INNER = 24 * 2**20
VMEM_OUTER = 24 * 2**20
WHOLE = pl.BlockSpec(memory_space=pltpu.VMEM)


def render_inner(depth_rank, density, quarters):
    depth, rows, columns = density.shape
    band = rows // quarters
    middle = rows - 2 * band
    shapes = [(depth, 2 * band), (2, middle), (4, middle)]
    cells = depth * rows * columns
    return pl.pallas_call(
        inner_kernel,
        in_specs=[pl.BlockSpec(memory_space=pltpu.SMEM), pl.BlockSpec(memory_space=pltpu.HBM)],
        out_specs=[WHOLE] * 4,
        out_shape=[pltpu.VMEM(density.shape, density.dtype)]
        + [pltpu.VMEM((a, b, columns), jnp.float32) for a, b in shapes],
        scratch_shapes=[pltpu.VMEM((depth, middle, XB), jnp.float32)] * 2
        + [
            pltpu.VMEM((2 * rows, 4 * rows), density.dtype),
            pltpu.VMEM((XB, XB), density.dtype),
            pltpu.VMEM((3, XB, XB), density.dtype),
            pltpu.SemaphoreType.DMA((columns // XB,)),
        ],
        compiler_params=pltpu.CompilerParams(vmem_limit_bytes=VMEM_INNER),
        cost_estimate=pl.CostEstimate(
            flops=1000 * cells, bytes_accessed=8 * cells, transcendentals=5 * cells
        ),
        name="inner",
    )(depth_rank, pltpu.with_memory_space_constraint(density, pltpu.HBM))


def render_outer(depth_rank, inner, halos, k, quarters):
    depth, rows, columns = inner[0].shape
    band = rows // quarters
    cells = depth * band * columns
    return pl.pallas_call(
        functools.partial(outer_kernel, k),
        in_specs=[pl.BlockSpec(memory_space=pltpu.SMEM)] + [WHOLE] * 8,
        out_specs=WHOLE,
        out_shape=pltpu.VMEM((2, band, columns), jnp.int32),
        scratch_shapes=[pltpu.VMEM((depth, 8, LANES), jnp.float32)],
        compiler_params=pltpu.CompilerParams(vmem_limit_bytes=VMEM_OUTER),
        cost_estimate=pl.CostEstimate(
            flops=1000 * cells, bytes_accessed=8 * cells, transcendentals=5 * cells
        ),
        name="outer%d" % k,
    )(depth_rank, *inner, *halos)


def decode(words):
    low = (words & 65535).astype(jnp.float32) * (1.0 / CODE)
    high = ((words >> 16) & 65535).astype(jnp.float32) * (1.0 / CODE)
    return low, high


def tile_bytes(value):
    code = jnp.floor(value * CODE + 0.5)
    high = jnp.floor(code * (1.0 / 256.0))
    return high.astype(jnp.bfloat16), (code - 256.0 * high).astype(jnp.bfloat16)


def gather_kernel(rank, home, *refs):
    bricks, out = refs[:-1], refs[-1]
    members = len(bricks)
    _, band, columns = bricks[0].shape
    across = columns // PIECE
    count = band * across
    ascend = rank[0] == 0
    me = lax.axis_index("depth")
    places = []
    for k in range(members):
        index = lax.rem(me - k + members, members)
        places.append(jnp.where(ascend, index, members - 1 - index))

    piece = lax.broadcasted_iota(jnp.int32, (count, count), 0)
    column = lax.broadcasted_iota(jnp.int32, (count, count), 1)
    homes = home[...]
    regroup = (piece == lax.rem(column, band) * across + column // band).astype(jnp.bfloat16)
    named = (piece == (homes // count)).astype(jnp.bfloat16)
    earlier = dot(named, (piece < column).astype(jnp.bfloat16))
    slots = (homes % count + 1).astype(jnp.float32)
    label = jnp.zeros((count, 128), jnp.int32)
    lane = lax.broadcasted_iota(jnp.int32, (count, 128), 1)
    routes = []
    for e in range(2):
        chosen = named.astype(jnp.float32) * (earlier == float(e)).astype(jnp.float32)
        here = jnp.sum(chosen * slots, axis=1, keepdims=True).astype(jnp.int32)
        label = label + jnp.where(lane == e, here, 0)
        routes.append(dot(chosen.astype(jnp.bfloat16), regroup).astype(jnp.bfloat16))
    out[:, 2 * PAYLOAD :] = label

    planes = [[], [], []]
    for c in range(across):
        part = slice(c * PIECE, (c + 1) * PIECE)
        colors, clears = [], []
        for brick in bricks:
            first, second = decode(brick[0, :, part])
            third, clear = decode(brick[1, :, part])
            colors.append((first, second, third))
            clears.append(clear)
        total = clears[0]
        for clear in clears[1:]:
            total = total * clear
        done = [total * b for b in BACKDROP]
        for k in range(members):
            ahead = None
            for other in range(members):
                if other != k:
                    factor = jnp.where(places[other] < places[k], clears[other], 1.0)
                    ahead = factor if ahead is None else ahead * factor
            done = [d + ahead * color for d, color in zip(done, colors[k])]
        for channel in range(3):
            planes[channel].append(tile_bytes(done[channel]))
    for channel in range(3):
        high = jnp.concatenate([p[0] for p in planes[channel]], 0)
        low = jnp.concatenate([p[1] for p in planes[channel]], 0)
        for e in range(2):
            code = (256.0 * dot(routes[e], high) + dot(routes[e], low)).astype(jnp.int32)
            words = code[:, :HALF] + (code[:, HALF:] << 16)
            at = e * PAYLOAD + channel * HALF
            out[:, at : at + HALF] = words


def gather(depth_rank, piece_home, bricks):
    _, band, columns = bricks[0].shape
    count = piece_home.shape[0]
    vmem = pl.BlockSpec(memory_space=pltpu.VMEM)
    return pl.pallas_call(
        gather_kernel,
        in_specs=[pl.BlockSpec(memory_space=pltpu.SMEM)] + [vmem] * (1 + len(bricks)),
        out_specs=vmem,
        out_shape=jax.ShapeDtypeStruct((count, ROW_WORDS), jnp.int32),
        compiler_params=pltpu.CompilerParams(vmem_limit_bytes=24 * 2**20),
        name="gather",
    )(depth_rank, piece_home.reshape(1, count), *bricks)


def place_kernel(arrived, out):
    count = arrived.shape[0]
    slot = lax.broadcasted_iota(jnp.int32, (count, count), 1)
    choices = [
        (arrived[:, 2 * PAYLOAD + e : 2 * PAYLOAD + e + 1] == slot + 1).astype(jnp.bfloat16)
        for e in range(2)
    ]
    choice = jnp.concatenate(choices, 0)

    def plane(words, shift):
        return ((words >> shift) & 255).astype(jnp.float32).astype(jnp.bfloat16)

    def put(planes):
        return lax.dot_general(
            choice, planes, (((0,), (0,)), ((), ())), preferred_element_type=jnp.float32
        )

    for channel in range(3):
        at = channel * HALF
        words = jnp.concatenate(
            [arrived[:, e * PAYLOAD + at : e * PAYLOAD + at + HALF] for e in range(2)], 0
        )
        for half in range(2):
            code = 256.0 * put(plane(words, 16 * half + 8)) + put(plane(words, 16 * half))
            out[channel, 0, :, half * HALF : (half + 1) * HALF] = code * (1.0 / CODE)


def place(arrived):
    count = arrived.shape[0]
    vmem = pl.BlockSpec(memory_space=pltpu.VMEM)
    return pl.pallas_call(
        place_kernel,
        in_specs=[vmem],
        out_specs=vmem,
        out_shape=jax.ShapeDtypeStruct((3, 1, count, PIECE), jnp.float32),
        compiler_params=pltpu.CompilerParams(vmem_limit_bytes=24 * 2**20),
        name="place",
    )(arrived)


def from_neighbors(first, last, axis):
    peers = lax.axis_size(axis)
    up = [(i, i + 1) for i in range(peers - 1)]
    return lax.ppermute(last, axis, up), lax.ppermute(first, axis, [(b, a) for a, b in up])


def on_device(density, depth_rank, piece_home):
    members = lax.axis_size("depth")
    below, above = from_neighbors(density[:1], density[-1:], "depth")
    front, back = from_neighbors(density[:, 0], density[:, -1], "tile")
    inner = render_inner(depth_rank, density, members)
    halos = (below, above, front, back)
    bricks = [None] * members
    for k in sorted(range(members), key=lambda k: (k == 0, -min(k, members - k), k)):
        part = render_outer(depth_rank, inner, halos, k, members)
        ring = [(i, (i + k) % members) for i in range(members)]
        bricks[k] = lax.ppermute(part, "depth", ring) if k else part
    outbox = gather(depth_rank, piece_home, bricks)
    arrived = lax.all_to_all(outbox, "tile", split_axis=0, concat_axis=0, tiled=True)
    return place(arrived)


def solution(mesh):
    in_specs = (P("depth", "tile", None), P(), P("tile"))
    out_specs = P(None, "depth", "tile", None)
    return jax.shard_map(
        on_device, mesh=mesh, in_specs=in_specs, out_specs=out_specs, check_vma=False
    )
```

```python
import functools
import math

import jax
import jax.numpy as jnp
import numpy as np
from jax import lax
from jax.experimental import pallas as pl
from jax.experimental.pallas import tpu as pltpu
from jax.sharding import PartitionSpec as P

EXTINCT = 0.5
BACKDROP = (0.08, 0.1, 0.14)
CODE = 65535.0

XB = 256
PIECE = 512
HALF = PIECE // 2
PAYLOAD = 3 * HALF
ROW_WORDS = 2 * PAYLOAD + 128


def cosine_polynomial(degree):
    limit = (0.85 * math.log(0.01) + math.pi / 2) ** 2 * 1.0005
    nodes = np.cos(np.pi * (np.arange(4000) + 0.5) / 4000)
    points = (nodes + 1) * limit / 2
    fit = np.polynomial.chebyshev.Chebyshev.fit(
        points, np.cos(np.sqrt(points)), degree, domain=[0, limit]
    )
    return [float(c) for c in fit.convert(kind=np.polynomial.Polynomial).coef]


COS = cosine_polynomial(4)
SHIFT = math.exp(math.pi / 1.7)
OFFSET = 0.01 * SHIFT
EXTINCT2 = -0.5 * math.log2(math.e) / SHIFT
NEAR = SHIFT * math.exp(-3.0)
FAR = SHIFT * math.exp(-2.5)
MONIC = [COS[i] / COS[4] / 0.85 ** (8 - 2 * i) for i in range(4)]
COSINE_SCALE = (COS[4] * 0.85**8) ** 2


def difference_matrices(along_zy, along_x, beside):
    def bands(ref, shape, pairs):
        row = lax.broadcasted_iota(jnp.int32, shape, 0)
        column = lax.broadcasted_iota(jnp.int32, shape, 1)
        total = jnp.zeros(shape, jnp.float32)
        for value, where in pairs:
            total = jnp.where(where(row, column), value, total)
        ref[...] = total.astype(ref.dtype)

    bands(
        along_x,
        (XB, XB),
        ((16.0, lambda i, j: i == j + 1), (-16.0, lambda i, j: i + 1 == j)),
    )
    left = (-16.0, lambda i, j: (i == 127) & (j == 0))
    right = (16.0, lambda i, j: (i == 128) & (j == XB - 1))
    for n, pairs in enumerate(((right,), (left, right), (left,))):
        bands(beside.at[n], (XB, XB), pairs)
    rows = along_zy.shape[0] // 2
    inside = lambda i: lax.rem(i, rows)
    bands(
        along_zy,
        (2 * rows, 4 * rows),
        (
            (15.0, lambda i, j: j == i + 2 * rows),
            (-15.0, lambda i, j: j == i),
            (12.0, lambda i, j: (j == i + rows + 1) & (inside(i) < rows - 1)),
            (-12.0, lambda i, j: (j == i + rows - 1) & (inside(i) > 0)),
        ),
    )


def dot(a, b):
    return jnp.dot(a, b, preferred_element_type=jnp.float32)


def encode(value):
    return (value * CODE + 0.5).astype(jnp.int32)


def shade(facing_sum, density, weight):
    weight = weight * (jnp.tanh(0.12 * facing_sum) + 0.675 / 0.325)
    logged = jnp.log(density + OFFSET)
    square = logged * logged
    c0, c1, c2, c3 = MONIC
    cosine = (((square + c3) * square + c2) * square + c1) * square + c0
    near = pltpu.reciprocal(density + (OFFSET + NEAR))
    far = pltpu.reciprocal(density + (OFFSET + FAR))
    return weight, weight * near, weight * (cosine * cosine), weight * far


def colors_of(plain, sum0, sum1, sum2):
    plain = 0.325 * plain
    return plain - (0.325 * NEAR) * sum0, plain - (0.325 * COSINE_SCALE) * sum1, (0.325 * FAR) * sum2


def scaled(cells):
    return SHIFT * cells.astype(jnp.float32)


def advance(z, cell, slope, carry):
    total, clear, *sums = carry
    density = cell(z)
    total = total + density
    after = jnp.exp2(EXTINCT2 * total)
    terms = shade(slope(z), density, clear - after)
    return (total, after, *(s + t for s, t in zip(sums, terms)))


def behind_first(start):
    zero = jnp.zeros_like(start)
    return start, jnp.exp2(EXTINCT2 * start), zero, zero, zero, zero


def march(cell, slope, ascend, first, last, start, unroll):
    def step(i, carry):
        return advance(jnp.where(ascend, first + i, last - i), cell, slope, carry)

    return lax.fori_loop(0, last - first + 1, step, behind_first(start), unroll=unroll)


SEGMENT = 8
INNER_ROWS = (8, 40)
OUTER_ROWS = ((0, 8), (24, 16), (56, 8))
LANES = 128
UNROLL_OUTER = 30


def inner_kernel(
    rank, density, cells, edge, layers, part, slope0, slope1, along_zy, along_x, beside, arrivals
):
    slopes = (slope0, slope1)
    depth, rows, columns = cells.shape
    band = edge.shape[1] // 2
    blocks = columns // XB
    ascend = rank[0] == 0
    begin = jnp.where(ascend, 0, depth - 1)
    tiles = [
        (row, lane) for row in range(0, rows - 2 * band, band) for lane in range(0, XB, LANES)
    ]
    chunk = SEGMENT

    def arrival(block):
        lanes = pl.ds(pl.multiple_of(block * XB, XB), XB)
        return pltpu.make_async_copy(
            density.at[:, :, lanes], cells.at[:, :, lanes], arrivals.at[block]
        )

    def differences(block, n, slope):
        lanes = pl.ds(pl.multiple_of(block * XB, XB), XB)
        left = pl.ds(pl.multiple_of(jnp.maximum(block * XB - 128, 0), 128), 128)
        right = pl.ds(pl.multiple_of(jnp.minimum(block * XB + XB, columns - 128), 128), 128)
        kind = jnp.where(block == 0, 0, jnp.where(block == blocks - 1, 2, 1))
        span = slice(n * chunk, (n + 1) * chunk)
        flat = lambda at: cells[span, :, at].reshape(chunk * rows, -1)
        sides = jnp.concatenate([flat(left), flat(right)], 1)
        across = dot(flat(lanes), along_x[...]) + dot(sides, beside[kind])
        nothing = jnp.zeros((1, rows, XB), cells.dtype)
        found = []
        for pair in range(0, chunk, 2):
            z = n * chunk + pair
            low = nothing if z == 0 else cells[z - 1 : z, :, lanes]
            high = nothing if z + 2 == depth else cells[z + 2 : z + 3, :, lanes]
            stack = jnp.concatenate([low, cells[z : z + 2, :, lanes], high], 0)
            both = across[pair * rows : (pair + 2) * rows] + dot(
                along_zy[...], stack.reshape(4 * rows, XB)
            )
            found.append((z, both.reshape(2, rows, XB)))
        return found

    def keep(block, found, slope):
        lanes = pl.ds(pl.multiple_of(block * XB, XB), XB)
        for z, both in found:
            at = 0
            for first, rest in OUTER_ROWS:
                edge[z : z + 2, at : at + rest, lanes] = both[:, first : first + rest]
                at += rest
            for n, first in enumerate(INNER_ROWS):
                here = slice(n * band, (n + 1) * band)
                slope[z : z + 2, here] = both[:, first : first + band]
                if z == 0:
                    layers[0, here, lanes] = both[0, first : first + band]
                if z + 2 == depth:
                    layers[1, here, lanes] = both[1, first : first + band]

    def rays(block, slope):
        for row, lane in tiles:
            lanes = pl.ds(pl.multiple_of(block * XB + lane, 128), LANES)
            here = slice(row, row + band)
            start = INNER_ROWS[row // band] - band // 2
            upper, lower = slice(start, start + band), slice(start + band, start + 2 * band)

            def cell(z):
                halves = (
                    cells[z, upper, lanes].astype(jnp.float32)[band // 2 :],
                    cells[z, lower, lanes].astype(jnp.float32)[: band // 2],
                )
                return SHIFT * jnp.concatenate(halves, 0)

            facing = lambda z: slope[z, here, lane : lane + LANES]
            carry = behind_first(cell(begin))
            for i in range(1, depth - 1):
                carry = advance(jnp.where(ascend, i, depth - 1 - i), cell, facing, carry)
                if i < depth - 2:
                    yield
            total, _, *sums = carry
            total = total + cell(depth - 1 - begin)
            for n, color in enumerate(colors_of(*sums)):
                part[n, here, lanes] = color
            part[3, here, lanes] = jnp.exp2(EXTINCT2 * total)
            yield

    def both(ahead, behind, parity):
        cells_left = iter(()) if behind is None else rays(behind, slopes[1 - parity])
        segments = depth // chunk
        steps = (depth - 2) * len(tiles)
        for n in range(segments):
            found = [] if ahead is None else differences(ahead, n, slopes[parity])
            for _ in range(steps * (n + 1) // segments - steps * n // segments):
                next(cells_left, None)
            keep(ahead, found, slopes[parity]) if found else None

    for block in range(blocks):
        arrival(block).start()
    difference_matrices(along_zy, along_x, beside)
    arrival(0).wait()
    arrival(1).wait()
    both(0, None, 0)

    @pl.loop(0, blocks // 2 - 1)
    def _(pair):
        arrival(2 * pair + 2).wait()
        both(2 * pair + 1, 2 * pair, 1)
        arrival(2 * pair + 3).wait()
        both(2 * pair + 2, 2 * pair + 1, 0)

    both(blocks - 1, blocks - 2, 1)
    both(None, blocks - 1, 0)


def outer_kernel(k, rank, cells, edge, layers, part, below, above, front, back, out, ends):
    depth, rows, columns = cells.shape
    _, band, _ = out.shape
    quarters = rows // band
    ascend = rank[0] == 0
    band_index = lax.rem(lax.axis_index("depth") + k, quarters)
    here = pl.ds(pl.multiple_of(band_index * band, band), band)
    begin = jnp.where(ascend, 0, depth - 1)
    half = band // 2
    mine = pl.ds(pl.multiple_of(band_index * half, half), half)
    line = lax.broadcasted_iota(jnp.int32, (half, WIDE), 0)

    def run(odd):
        pick = (lambda v: v[half:]) if odd else (lambda v: v[:half])
        merge = lambda here, there: jnp.concatenate([there, here] if odd else [here, there], 0)
        if odd:
            halo, edge_line = back, half - 1
            factor = jnp.where(band_index == quarters - 1, 12.0, 0.0)
        else:
            halo, edge_line = front, 0
            factor = jnp.where(band_index == 0, -12.0, 0.0)

        @pl.loop(0, columns // WIDE)
        def _(column):
            lanes = pl.ds(pl.multiple_of(column * WIDE, WIDE), WIDE)
            whole = lambda z: cells[z, here, lanes].astype(jnp.float32)
            cell = lambda z: SHIFT * pick(whole(z))
            lines = factor * halo[:, lanes].astype(jnp.float32)
            for z in range(depth):
                ends[z] = jnp.where(line == edge_line, lines[z : z + 1], 0.0)
            slope = lambda z: edge[z, mine, lanes] + ends[z]
            total, _, *sums = march(
                cell, slope, ascend, 1, depth - 2, cell(begin), UNROLL_OUTER
            )
            through = jnp.exp2(EXTINCT2 * (total + cell(depth - 1 - begin)))
            through = merge(through, part[3, mine, lanes])
            colors = [
                merge(color, part[n, mine, lanes]) for n, color in enumerate(colors_of(*sums))
            ]
            sums = None
            for n, z, sign, beyond in ((0, 0, -15.0, below), (1, depth - 1, 15.0, above)):
                density = SHIFT * whole(z)
                clear = jnp.exp2(EXTINCT2 * density)
                nearest = ascend if n == 0 else jnp.logical_not(ascend)
                weight = jnp.where(nearest, 1.0 - clear, through / clear - through)
                facing = merge(slope(z), layers[n, mine, lanes])
                facing = facing + sign * beyond[0, here, lanes].astype(jnp.float32)
                terms = shade(facing, density, weight)
                sums = terms if sums is None else [s + t for s, t in zip(sums, terms)]
            done = [c + d for c, d in zip(colors, colors_of(*sums))]
            out[0, :, lanes] = encode(done[0]) + (encode(done[1]) << 16)
            out[1, :, lanes] = encode(done[2]) + (encode(through) << 16)

    pl.when(lax.rem(band_index, 2) == 0)(lambda: run(False))
    pl.when(lax.rem(band_index, 2) == 1)(lambda: run(True))


WIDE = 256
VMEM_INNER = 24 * 2**20
VMEM_OUTER = 24 * 2**20
WHOLE = pl.BlockSpec(memory_space=pltpu.VMEM)


def render_inner(depth_rank, density, quarters):
    depth, rows, columns = density.shape
    band = rows // quarters
    middle = rows - 2 * band
    shapes = [(depth, 2 * band), (2, middle), (4, middle)]
    cells = depth * rows * columns
    return pl.pallas_call(
        inner_kernel,
        in_specs=[pl.BlockSpec(memory_space=pltpu.SMEM), pl.BlockSpec(memory_space=pltpu.HBM)],
        out_specs=[WHOLE] * 4,
        out_shape=[pltpu.VMEM(density.shape, density.dtype)]
        + [pltpu.VMEM((a, b, columns), jnp.float32) for a, b in shapes],
        scratch_shapes=[pltpu.VMEM((depth, middle, XB), jnp.float32)] * 2
        + [
            pltpu.VMEM((2 * rows, 4 * rows), density.dtype),
            pltpu.VMEM((XB, XB), density.dtype),
            pltpu.VMEM((3, XB, XB), density.dtype),
            pltpu.SemaphoreType.DMA((columns // XB,)),
        ],
        compiler_params=pltpu.CompilerParams(vmem_limit_bytes=VMEM_INNER),
        cost_estimate=pl.CostEstimate(
            flops=1000 * cells, bytes_accessed=8 * cells, transcendentals=5 * cells
        ),
        name="inner",
    )(depth_rank, pltpu.with_memory_space_constraint(density, pltpu.HBM))


def render_outer(depth_rank, inner, halos, k, quarters):
    depth, rows, columns = inner[0].shape
    band = rows // quarters
    cells = depth * band * columns
    return pl.pallas_call(
        functools.partial(outer_kernel, k),
        in_specs=[pl.BlockSpec(memory_space=pltpu.SMEM)] + [WHOLE] * 8,
        out_specs=WHOLE,
        out_shape=pltpu.VMEM((2, band, columns), jnp.int32),
        scratch_shapes=[pltpu.VMEM((depth, band // 2, WIDE), jnp.float32)],
        compiler_params=pltpu.CompilerParams(vmem_limit_bytes=VMEM_OUTER),
        cost_estimate=pl.CostEstimate(
            flops=1000 * cells, bytes_accessed=8 * cells, transcendentals=5 * cells
        ),
        name="outer%d" % k,
    )(depth_rank, *inner, *halos)


def decode(words):
    low = (words & 65535).astype(jnp.float32) * (1.0 / CODE)
    high = ((words >> 16) & 65535).astype(jnp.float32) * (1.0 / CODE)
    return low, high


def tile_bytes(value):
    code = jnp.floor(value * CODE + 0.5)
    high = jnp.floor(code * (1.0 / 256.0))
    return high.astype(jnp.bfloat16), (code - 256.0 * high).astype(jnp.bfloat16)


def gather_kernel(rank, home, *refs):
    bricks, out = refs[:-1], refs[-1]
    members = len(bricks)
    _, band, columns = bricks[0].shape
    across = columns // PIECE
    count = band * across
    ascend = rank[0] == 0
    me = lax.axis_index("depth")
    places = []
    for k in range(members):
        index = lax.rem(me - k + members, members)
        places.append(jnp.where(ascend, index, members - 1 - index))

    piece = lax.broadcasted_iota(jnp.int32, (count, count), 0)
    column = lax.broadcasted_iota(jnp.int32, (count, count), 1)
    homes = home[...]
    regroup = (piece == lax.rem(column, band) * across + column // band).astype(jnp.bfloat16)
    named = (piece == (homes // count)).astype(jnp.bfloat16)
    earlier = dot(named, (piece < column).astype(jnp.bfloat16))
    slots = (homes % count + 1).astype(jnp.float32)
    label = jnp.zeros((count, 128), jnp.int32)
    lane = lax.broadcasted_iota(jnp.int32, (count, 128), 1)
    routes = []
    for e in range(2):
        chosen = named.astype(jnp.float32) * (earlier == float(e)).astype(jnp.float32)
        here = jnp.sum(chosen * slots, axis=1, keepdims=True).astype(jnp.int32)
        label = label + jnp.where(lane == e, here, 0)
        routes.append(dot(chosen.astype(jnp.bfloat16), regroup).astype(jnp.bfloat16))
    out[:, 2 * PAYLOAD :] = label

    planes = [[], [], []]
    for c in range(across):
        part = slice(c * PIECE, (c + 1) * PIECE)
        colors, clears = [], []
        for brick in bricks:
            first, second = decode(brick[0, :, part])
            third, clear = decode(brick[1, :, part])
            colors.append((first, second, third))
            clears.append(clear)
        total = clears[0]
        for clear in clears[1:]:
            total = total * clear
        done = [total * b for b in BACKDROP]
        for k in range(members):
            ahead = None
            for other in range(members):
                if other != k:
                    factor = jnp.where(places[other] < places[k], clears[other], 1.0)
                    ahead = factor if ahead is None else ahead * factor
            done = [d + ahead * color for d, color in zip(done, colors[k])]
        for channel in range(3):
            planes[channel].append(tile_bytes(done[channel]))
    for channel in range(3):
        high = jnp.concatenate([p[0] for p in planes[channel]], 0)
        low = jnp.concatenate([p[1] for p in planes[channel]], 0)
        for e in range(2):
            code = (256.0 * dot(routes[e], high) + dot(routes[e], low)).astype(jnp.int32)
            words = code[:, :HALF] + (code[:, HALF:] << 16)
            at = e * PAYLOAD + channel * HALF
            out[:, at : at + HALF] = words


def gather(depth_rank, piece_home, bricks):
    _, band, columns = bricks[0].shape
    count = piece_home.shape[0]
    vmem = pl.BlockSpec(memory_space=pltpu.VMEM)
    return pl.pallas_call(
        gather_kernel,
        in_specs=[pl.BlockSpec(memory_space=pltpu.SMEM)] + [vmem] * (1 + len(bricks)),
        out_specs=vmem,
        out_shape=jax.ShapeDtypeStruct((count, ROW_WORDS), jnp.int32),
        compiler_params=pltpu.CompilerParams(vmem_limit_bytes=24 * 2**20),
        name="gather",
    )(depth_rank, piece_home.reshape(1, count), *bricks)


def place_kernel(arrived, out):
    count = arrived.shape[0]
    slot = lax.broadcasted_iota(jnp.int32, (count, count), 1)
    choices = [
        (arrived[:, 2 * PAYLOAD + e : 2 * PAYLOAD + e + 1] == slot + 1).astype(jnp.bfloat16)
        for e in range(2)
    ]
    choice = jnp.concatenate(choices, 0)

    def plane(words, shift):
        return ((words >> shift) & 255).astype(jnp.float32).astype(jnp.bfloat16)

    def put(planes):
        return lax.dot_general(
            choice, planes, (((0,), (0,)), ((), ())), preferred_element_type=jnp.float32
        )

    for channel in range(3):
        at = channel * HALF
        words = jnp.concatenate(
            [arrived[:, e * PAYLOAD + at : e * PAYLOAD + at + HALF] for e in range(2)], 0
        )
        for half in range(2):
            code = 256.0 * put(plane(words, 16 * half + 8)) + put(plane(words, 16 * half))
            out[channel, 0, :, half * HALF : (half + 1) * HALF] = code * (1.0 / CODE)


def place(arrived):
    count = arrived.shape[0]
    vmem = pl.BlockSpec(memory_space=pltpu.VMEM)
    return pl.pallas_call(
        place_kernel,
        in_specs=[vmem],
        out_specs=vmem,
        out_shape=jax.ShapeDtypeStruct((3, 1, count, PIECE), jnp.float32),
        compiler_params=pltpu.CompilerParams(vmem_limit_bytes=24 * 2**20),
        name="place",
    )(arrived)


def from_neighbors(first, last, axis):
    peers = lax.axis_size(axis)
    up = [(i, i + 1) for i in range(peers - 1)]
    return lax.ppermute(last, axis, up), lax.ppermute(first, axis, [(b, a) for a, b in up])


def on_device(density, depth_rank, piece_home):
    members = lax.axis_size("depth")
    below, above = from_neighbors(density[:1], density[-1:], "depth")
    front, back = from_neighbors(density[:, 0], density[:, -1], "tile")
    inner = render_inner(depth_rank, density, members)
    halos = (below, above, front, back)
    bricks = [None] * members
    for k in sorted(range(members), key=lambda k: (k == 0, -min(k, members - k), k)):
        part = render_outer(depth_rank, inner, halos, k, members)
        ring = [(i, (i + k) % members) for i in range(members)]
        bricks[k] = lax.ppermute(part, "depth", ring) if k else part
    outbox = gather(depth_rank, piece_home, bricks)
    arrived = lax.all_to_all(outbox, "tile", split_axis=0, concat_axis=0, tiled=True)
    return place(arrived)


def solution(mesh):
    in_specs = (P("depth", "tile", None), P(), P("tile"))
    out_specs = P(None, "depth", "tile", None)
    return jax.shard_map(
        on_device, mesh=mesh, in_specs=in_specs, out_specs=out_specs, check_vma=False
    )
```

```python
import functools
import math

import jax
import jax.numpy as jnp
import numpy as np
from jax import lax
from jax.experimental import pallas as pl
from jax.experimental.pallas import tpu as pltpu
from jax.sharding import PartitionSpec as P

EXTINCT = 0.5
BACKDROP = (0.08, 0.1, 0.14)
CODE = 65535.0

XB = 256
PIECE = 512
HALF = PIECE // 2
PAYLOAD = 3 * HALF
ROW_WORDS = 2 * PAYLOAD + 128


def cosine_polynomial(degree):
    limit = (0.85 * math.log(0.01) + math.pi / 2) ** 2 * 1.0005
    nodes = np.cos(np.pi * (np.arange(4000) + 0.5) / 4000)
    points = (nodes + 1) * limit / 2
    fit = np.polynomial.chebyshev.Chebyshev.fit(
        points, np.cos(np.sqrt(points)), degree, domain=[0, limit]
    )
    return [float(c) for c in fit.convert(kind=np.polynomial.Polynomial).coef]


COS = cosine_polynomial(4)
SHIFT = math.exp(math.pi / 1.7)
OFFSET = 0.01 * SHIFT
EXTINCT2 = -0.5 * math.log2(math.e) / SHIFT
NEAR = SHIFT * math.exp(-3.0)
FAR = SHIFT * math.exp(-2.5)
MONIC = [COS[i] / COS[4] / 0.85 ** (8 - 2 * i) for i in range(4)]
COSINE_SCALE = (COS[4] * 0.85**8) ** 2


def difference_matrices(along_zy, along_x):
    def bands(ref, shape, pairs):
        row = lax.broadcasted_iota(jnp.int32, shape, 0)
        column = lax.broadcasted_iota(jnp.int32, shape, 1)
        total = jnp.zeros(shape, jnp.float32)
        for value, where in pairs:
            total = jnp.where(where(row, column), value, total)
        ref[...] = total.astype(ref.dtype)

    bands(
        along_x,
        (XB, XB),
        ((16.0, lambda i, j: i == j + 1), (-16.0, lambda i, j: i + 1 == j)),
    )
    rows = along_zy.shape[0] // 2
    inside = lambda i: lax.rem(i, rows)
    bands(
        along_zy,
        (2 * rows, 4 * rows),
        (
            (15.0, lambda i, j: j == i + 2 * rows),
            (-15.0, lambda i, j: j == i),
            (12.0, lambda i, j: (j == i + rows + 1) & (inside(i) < rows - 1)),
            (-12.0, lambda i, j: (j == i + rows - 1) & (inside(i) > 0)),
        ),
    )


def dot(a, b):
    return jnp.dot(a, b, preferred_element_type=jnp.float32)


def encode(value):
    return (value * CODE + 0.5).astype(jnp.int32)


def shade(facing_sum, density, weight):
    weight = weight * (jnp.tanh(0.12 * facing_sum) + 0.675 / 0.325)
    logged = jnp.log(density + OFFSET)
    square = logged * logged
    c0, c1, c2, c3 = MONIC
    cosine = (((square + c3) * square + c2) * square + c1) * square + c0
    near = pltpu.reciprocal(density + (OFFSET + NEAR))
    far = pltpu.reciprocal(density + (OFFSET + FAR))
    return weight, weight * near, weight * (cosine * cosine), weight * far


def colors_of(plain, sum0, sum1, sum2):
    plain = 0.325 * plain
    return plain - (0.325 * NEAR) * sum0, plain - (0.325 * COSINE_SCALE) * sum1, (0.325 * FAR) * sum2


def scaled(cells):
    return SHIFT * cells.astype(jnp.float32)


def advance(z, cell, slope, carry):
    total, clear, *sums = carry
    density = cell(z)
    total = total + density
    after = jnp.exp2(EXTINCT2 * total)
    terms = shade(slope(z), density, clear - after)
    return (total, after, *(s + t for s, t in zip(sums, terms)))


def behind_first(start):
    zero = jnp.zeros_like(start)
    return start, jnp.exp2(EXTINCT2 * start), zero, zero, zero, zero


def march(cell, slope, ascend, first, last, start, unroll):
    def step(i, carry):
        return advance(jnp.where(ascend, first + i, last - i), cell, slope, carry)

    return lax.fori_loop(0, last - first + 1, step, behind_first(start), unroll=unroll)


SEGMENT = 4
INNER_ROWS = (8, 40)
OUTER_ROWS = ((0, 8), (24, 16), (56, 8))
LANES = 128
UNROLL_OUTER = 30


def inner_kernel(
    rank, density, cells, edge, layers, part, slope0, slope1, along_zy, along_x, arrivals
):
    slopes = (slope0, slope1)
    depth, rows, columns = cells.shape
    band = edge.shape[1] // 2
    blocks = columns // XB
    ascend = rank[0] == 0
    begin = jnp.where(ascend, 0, depth - 1)
    tiles = [
        (row, lane) for row in range(0, rows - 2 * band, band) for lane in range(0, XB, LANES)
    ]
    chunk = SEGMENT
    lane128 = lax.broadcasted_iota(jnp.int32, (1, 128), 1)

    def arrival(block):
        lanes = pl.ds(pl.multiple_of(block * XB, XB), XB)
        return pltpu.make_async_copy(
            density.at[:, :, lanes], cells.at[:, :, lanes], arrivals.at[block]
        )

    def differences(block, n, slope):
        lanes = pl.ds(pl.multiple_of(block * XB, XB), XB)
        left = pl.ds(pl.multiple_of(jnp.maximum(block * XB - 128, 0), 128), 128)
        right = pl.ds(pl.multiple_of(jnp.minimum(block * XB + XB, columns - 128), 128), 128)
        span = slice(n * chunk, (n + 1) * chunk)
        flat = lambda at: cells[span, :, at].reshape(chunk * rows, -1)
        before = jnp.where((lane128 == 127) & (block > 0), -16.0, 0.0).astype(cells.dtype)
        beyond = jnp.where((lane128 == 0) & (block < blocks - 1), 16.0, 0.0).astype(cells.dtype)
        beside = [
            pltpu.roll((flat(at) * mask).astype(jnp.float32), shift, 1)
            for at, mask, shift in ((left, before, 1), (right, beyond, 127))
        ]
        across = dot(flat(lanes), along_x[...])
        across = jnp.concatenate([across[:, :128] + beside[0], across[:, 128:] + beside[1]], 1)
        nothing = jnp.zeros((1, rows, XB), cells.dtype)
        found = []
        for pair in range(0, chunk, 2):
            z = n * chunk + pair
            low = nothing if z == 0 else cells[z - 1 : z, :, lanes]
            high = nothing if z + 2 == depth else cells[z + 2 : z + 3, :, lanes]
            stack = jnp.concatenate([low, cells[z : z + 2, :, lanes], high], 0)
            both = across[pair * rows : (pair + 2) * rows] + dot(
                along_zy[...], stack.reshape(4 * rows, XB)
            )
            found.append((z, both.reshape(2, rows, XB)))
        return found

    def keep(block, found, slope):
        lanes = pl.ds(pl.multiple_of(block * XB, XB), XB)
        for z, both in found:
            at = 0
            for first, rest in OUTER_ROWS:
                edge[z : z + 2, at : at + rest, lanes] = both[:, first : first + rest]
                at += rest
            for n, first in enumerate(INNER_ROWS):
                here = slice(n * band, (n + 1) * band)
                slope[z : z + 2, here] = both[:, first : first + band]
                if z == 0:
                    layers[0, here, lanes] = both[0, first : first + band]
                if z + 2 == depth:
                    layers[1, here, lanes] = both[1, first : first + band]

    def rays(block, slope):
        for row, lane in tiles:
            lanes = pl.ds(pl.multiple_of(block * XB + lane, 128), LANES)
            here = slice(row, row + band)
            start = INNER_ROWS[row // band] - band // 2
            upper, lower = slice(start, start + band), slice(start + band, start + 2 * band)

            def cell(z):
                halves = (
                    cells[z, upper, lanes].astype(jnp.float32)[band // 2 :],
                    cells[z, lower, lanes].astype(jnp.float32)[: band // 2],
                )
                return SHIFT * jnp.concatenate(halves, 0)

            facing = lambda z: slope[z, here, lane : lane + LANES]
            carry = behind_first(cell(begin))
            for i in range(1, depth - 1):
                carry = advance(jnp.where(ascend, i, depth - 1 - i), cell, facing, carry)
                if i < depth - 2:
                    yield
            total, _, *sums = carry
            total = total + cell(depth - 1 - begin)
            for n, color in enumerate(colors_of(*sums)):
                part[n, here, lanes] = color
            part[3, here, lanes] = jnp.exp2(EXTINCT2 * total)
            yield

    def both(ahead, behind, parity):
        cells_left = iter(()) if behind is None else rays(behind, slopes[1 - parity])
        segments = depth // chunk
        steps = (depth - 2) * len(tiles)
        for n in range(segments):
            found = [] if ahead is None else differences(ahead, n, slopes[parity])
            for _ in range(steps * (n + 1) // segments - steps * n // segments):
                next(cells_left, None)
            keep(ahead, found, slopes[parity]) if found else None

    for block in range(blocks):
        arrival(block).start()
    difference_matrices(along_zy, along_x)
    arrival(0).wait()
    arrival(1).wait()
    both(0, None, 0)

    @pl.loop(0, blocks // 2 - 1)
    def _(pair):
        arrival(2 * pair + 2).wait()
        both(2 * pair + 1, 2 * pair, 1)
        arrival(2 * pair + 3).wait()
        both(2 * pair + 2, 2 * pair + 1, 0)

    both(blocks - 1, blocks - 2, 1)
    both(None, blocks - 1, 0)


def outer_kernel(k, rank, cells, edge, layers, part, below, above, front, back, out, ends):
    depth, rows, columns = cells.shape
    _, band, _ = out.shape
    quarters = rows // band
    ascend = rank[0] == 0
    band_index = lax.rem(lax.axis_index("depth") + k, quarters)
    here = pl.ds(pl.multiple_of(band_index * band, band), band)
    begin = jnp.where(ascend, 0, depth - 1)
    half = band // 2
    mine = pl.ds(pl.multiple_of(band_index * half, half), half)
    line = lax.broadcasted_iota(jnp.int32, (half, WIDE), 0)

    def run(odd):
        pick = (lambda v: v[half:]) if odd else (lambda v: v[:half])
        merge = lambda here, there: jnp.concatenate([there, here] if odd else [here, there], 0)
        if odd:
            halo, edge_line = back, half - 1
            factor = jnp.where(band_index == quarters - 1, 12.0, 0.0)
        else:
            halo, edge_line = front, 0
            factor = jnp.where(band_index == 0, -12.0, 0.0)

        @pl.loop(0, columns // WIDE)
        def _(column):
            lanes = pl.ds(pl.multiple_of(column * WIDE, WIDE), WIDE)
            whole = lambda z: cells[z, here, lanes].astype(jnp.float32)
            cell = lambda z: SHIFT * pick(whole(z))
            lines = factor * halo[:, lanes].astype(jnp.float32)
            for z in range(depth):
                ends[z] = jnp.where(line == edge_line, lines[z : z + 1], 0.0)
            slope = lambda z: edge[z, mine, lanes] + ends[z]
            total, _, *sums = march(
                cell, slope, ascend, 1, depth - 2, cell(begin), UNROLL_OUTER
            )
            through = jnp.exp2(EXTINCT2 * (total + cell(depth - 1 - begin)))
            through = merge(through, part[3, mine, lanes])
            colors = [
                merge(color, part[n, mine, lanes]) for n, color in enumerate(colors_of(*sums))
            ]
            sums = None
            for n, z, sign, beyond in ((0, 0, -15.0, below), (1, depth - 1, 15.0, above)):
                density = SHIFT * whole(z)
                clear = jnp.exp2(EXTINCT2 * density)
                nearest = ascend if n == 0 else jnp.logical_not(ascend)
                weight = jnp.where(nearest, 1.0 - clear, through / clear - through)
                facing = merge(slope(z), layers[n, mine, lanes])
                facing = facing + sign * beyond[0, here, lanes].astype(jnp.float32)
                terms = shade(facing, density, weight)
                sums = terms if sums is None else [s + t for s, t in zip(sums, terms)]
            done = [c + d for c, d in zip(colors, colors_of(*sums))]
            out[0, :, lanes] = encode(done[0]) + (encode(done[1]) << 16)
            out[1, :, lanes] = encode(done[2]) + (encode(through) << 16)

    pl.when(lax.rem(band_index, 2) == 0)(lambda: run(False))
    pl.when(lax.rem(band_index, 2) == 1)(lambda: run(True))


WIDE = 256
VMEM_INNER = 24 * 2**20
VMEM_OUTER = 24 * 2**20
WHOLE = pl.BlockSpec(memory_space=pltpu.VMEM)


def render_inner(depth_rank, density, quarters):
    depth, rows, columns = density.shape
    band = rows // quarters
    middle = rows - 2 * band
    shapes = [(depth, 2 * band), (2, middle), (4, middle)]
    cells = depth * rows * columns
    return pl.pallas_call(
        inner_kernel,
        in_specs=[pl.BlockSpec(memory_space=pltpu.SMEM), pl.BlockSpec(memory_space=pltpu.HBM)],
        out_specs=[WHOLE] * 4,
        out_shape=[pltpu.VMEM(density.shape, density.dtype)]
        + [pltpu.VMEM((a, b, columns), jnp.float32) for a, b in shapes],
        scratch_shapes=[pltpu.VMEM((depth, middle, XB), jnp.float32)] * 2
        + [
            pltpu.VMEM((2 * rows, 4 * rows), density.dtype),
            pltpu.VMEM((XB, XB), density.dtype),
            pltpu.SemaphoreType.DMA((columns // XB,)),
        ],
        compiler_params=pltpu.CompilerParams(vmem_limit_bytes=VMEM_INNER),
        cost_estimate=pl.CostEstimate(
            flops=1000 * cells, bytes_accessed=8 * cells, transcendentals=5 * cells
        ),
        name="inner",
    )(depth_rank, pltpu.with_memory_space_constraint(density, pltpu.HBM))


def render_outer(depth_rank, inner, halos, k, quarters):
    depth, rows, columns = inner[0].shape
    band = rows // quarters
    cells = depth * band * columns
    return pl.pallas_call(
        functools.partial(outer_kernel, k),
        in_specs=[pl.BlockSpec(memory_space=pltpu.SMEM)] + [WHOLE] * 8,
        out_specs=WHOLE,
        out_shape=pltpu.VMEM((2, band, columns), jnp.int32),
        scratch_shapes=[pltpu.VMEM((depth, band // 2, WIDE), jnp.float32)],
        compiler_params=pltpu.CompilerParams(vmem_limit_bytes=VMEM_OUTER),
        cost_estimate=pl.CostEstimate(
            flops=1000 * cells, bytes_accessed=8 * cells, transcendentals=5 * cells
        ),
        name="outer%d" % k,
    )(depth_rank, *inner, *halos)


def decode(words):
    low = (words & 65535).astype(jnp.float32) * (1.0 / CODE)
    high = ((words >> 16) & 65535).astype(jnp.float32) * (1.0 / CODE)
    return low, high


def tile_bytes(value):
    code = jnp.floor(value * CODE + 0.5)
    high = jnp.floor(code * (1.0 / 256.0))
    return high.astype(jnp.bfloat16), (code - 256.0 * high).astype(jnp.bfloat16)


def gather_kernel(rank, home, *refs):
    bricks, out = refs[:-1], refs[-1]
    members = len(bricks)
    _, band, columns = bricks[0].shape
    across = columns // PIECE
    count = band * across
    ascend = rank[0] == 0
    me = lax.axis_index("depth")
    places = []
    for k in range(members):
        index = lax.rem(me - k + members, members)
        places.append(jnp.where(ascend, index, members - 1 - index))

    piece = lax.broadcasted_iota(jnp.int32, (count, count), 0)
    column = lax.broadcasted_iota(jnp.int32, (count, count), 1)
    homes = home[...]
    regroup = (piece == lax.rem(column, band) * across + column // band).astype(jnp.bfloat16)
    named = (piece == (homes // count)).astype(jnp.bfloat16)
    earlier = dot(named, (piece < column).astype(jnp.bfloat16))
    slots = (homes % count + 1).astype(jnp.float32)
    label = jnp.zeros((count, 128), jnp.int32)
    lane = lax.broadcasted_iota(jnp.int32, (count, 128), 1)
    routes = []
    for e in range(2):
        chosen = named.astype(jnp.float32) * (earlier == float(e)).astype(jnp.float32)
        here = jnp.sum(chosen * slots, axis=1, keepdims=True).astype(jnp.int32)
        label = label + jnp.where(lane == e, here, 0)
        routes.append(dot(chosen.astype(jnp.bfloat16), regroup).astype(jnp.bfloat16))
    out[:, 2 * PAYLOAD :] = label

    planes = [[], [], []]
    for c in range(across):
        part = slice(c * PIECE, (c + 1) * PIECE)
        colors, clears = [], []
        for brick in bricks:
            first, second = decode(brick[0, :, part])
            third, clear = decode(brick[1, :, part])
            colors.append((first, second, third))
            clears.append(clear)
        total = clears[0]
        for clear in clears[1:]:
            total = total * clear
        done = [total * b for b in BACKDROP]
        for k in range(members):
            ahead = None
            for other in range(members):
                if other != k:
                    factor = jnp.where(places[other] < places[k], clears[other], 1.0)
                    ahead = factor if ahead is None else ahead * factor
            done = [d + ahead * color for d, color in zip(done, colors[k])]
        for channel in range(3):
            planes[channel].append(tile_bytes(done[channel]))
    for channel in range(3):
        high = jnp.concatenate([p[0] for p in planes[channel]], 0)
        low = jnp.concatenate([p[1] for p in planes[channel]], 0)
        for e in range(2):
            code = (256.0 * dot(routes[e], high) + dot(routes[e], low)).astype(jnp.int32)
            words = code[:, :HALF] + (code[:, HALF:] << 16)
            at = e * PAYLOAD + channel * HALF
            out[:, at : at + HALF] = words


def gather(depth_rank, piece_home, bricks):
    _, band, columns = bricks[0].shape
    count = piece_home.shape[0]
    vmem = pl.BlockSpec(memory_space=pltpu.VMEM)
    return pl.pallas_call(
        gather_kernel,
        in_specs=[pl.BlockSpec(memory_space=pltpu.SMEM)] + [vmem] * (1 + len(bricks)),
        out_specs=vmem,
        out_shape=jax.ShapeDtypeStruct((count, ROW_WORDS), jnp.int32),
        compiler_params=pltpu.CompilerParams(vmem_limit_bytes=24 * 2**20),
        name="gather",
    )(depth_rank, piece_home.reshape(1, count), *bricks)


def place_kernel(arrived, out):
    count = arrived.shape[0]
    slot = lax.broadcasted_iota(jnp.int32, (count, count), 1)
    choices = [
        (arrived[:, 2 * PAYLOAD + e : 2 * PAYLOAD + e + 1] == slot + 1).astype(jnp.bfloat16)
        for e in range(2)
    ]
    choice = jnp.concatenate(choices, 0)

    def plane(words, shift):
        return ((words >> shift) & 255).astype(jnp.float32).astype(jnp.bfloat16)

    def put(planes):
        return lax.dot_general(
            choice, planes, (((0,), (0,)), ((), ())), preferred_element_type=jnp.float32
        )

    for channel in range(3):
        at = channel * HALF
        words = jnp.concatenate(
            [arrived[:, e * PAYLOAD + at : e * PAYLOAD + at + HALF] for e in range(2)], 0
        )
        for half in range(2):
            code = 256.0 * put(plane(words, 16 * half + 8)) + put(plane(words, 16 * half))
            out[channel, 0, :, half * HALF : (half + 1) * HALF] = code * (1.0 / CODE)


def place(arrived):
    count = arrived.shape[0]
    vmem = pl.BlockSpec(memory_space=pltpu.VMEM)
    return pl.pallas_call(
        place_kernel,
        in_specs=[vmem],
        out_specs=vmem,
        out_shape=jax.ShapeDtypeStruct((3, 1, count, PIECE), jnp.float32),
        compiler_params=pltpu.CompilerParams(vmem_limit_bytes=24 * 2**20),
        name="place",
    )(arrived)


def from_neighbors(first, last, axis):
    peers = lax.axis_size(axis)
    up = [(i, i + 1) for i in range(peers - 1)]
    return lax.ppermute(last, axis, up), lax.ppermute(first, axis, [(b, a) for a, b in up])


def on_device(density, depth_rank, piece_home):
    members = lax.axis_size("depth")
    below, above = from_neighbors(density[:1], density[-1:], "depth")
    front, back = from_neighbors(density[:, 0], density[:, -1], "tile")
    inner = render_inner(depth_rank, density, members)
    halos = (below, above, front, back)
    bricks = [None] * members
    for k in sorted(range(members), key=lambda k: (k == 0, -min(k, members - k), k)):
        part = render_outer(depth_rank, inner, halos, k, members)
        ring = [(i, (i + k) % members) for i in range(members)]
        bricks[k] = lax.ppermute(part, "depth", ring) if k else part
    outbox = gather(depth_rank, piece_home, bricks)
    arrived = lax.all_to_all(outbox, "tile", split_axis=0, concat_axis=0, tiled=True)
    return place(arrived)


def solution(mesh):
    in_specs = (P("depth", "tile", None), P(), P("tile"))
    out_specs = P(None, "depth", "tile", None)
    return jax.shard_map(
        on_device, mesh=mesh, in_specs=in_specs, out_specs=out_specs, check_vma=False
    )
```
